128 devices in a mesh: dev: 128 (over z, y, x, core).
Axes of the slice: x: 4, y: 4, z: 4, core: 2. Of those that a mesh axis runs over, the one named last changes fastest.
Arguments:
- state: float32 [16384, 16, 512], P('dev'), may hold values from -6 to 6
- winds: float32 [2, 16384, 16, 128], P(None, 'dev'), may hold values from -3 to 3
- neighbours: int32 [16384, 8], P('dev'), may hold values from 0 to 16383, as said below
- valence: int32 [16384, 4], P('dev'), may hold values from 3 to 4, as said below
- cost: int32 [16384, 16], P('dev'), may hold values from 1 to 4, as said below
- w_in: bfloat16 [512, 384], replicated, may hold values from -0.375 to 0.375
- w_mid: bfloat16 [3, 384, 384], replicated, may hold values from -0.4375 to 0.4375
- w_out: bfloat16 [384, 512], replicated, may hold values from -0.625 to 0.625
Outputs:
- dyn_tend: float32 [16384, 16, 512], P('dev')
- phys_tend: bfloat16 [16384, 16, 512], P('dev')
The draws below stay inside these ranges and needn't reach their ends.
Inputs may be any that keep to these rules, and one draw needn't show every extreme that they name: Row g lists the curve positions of element g's neighbours across its +a, -a, +b, -b edges and at its (+a,+b), (+a,-b), (-a,+b), (-a,-b) corners. The curve is cut into sweeps of 16 consecutive positions starting at multiples of 16; the +b and -b neighbours lie in g's own sweep, the +a neighbour and the (+a,+b), (+a,-b) corner neighbours in the next sweep, the -a neighbour and the (-a,+b), (-a,-b) corner neighbours in the previous sweep, cyclically over 16384. The elements form a closed grid of quadrilaterals without rotations: an element is its neighbour's opposite neighbour. `valence`: corners in the order of the corner neighbours; all elements around one corner point agree. `cost`: regions of 128 consecutive elements along the curve share one cloud regime.
All inputs are finite; a program needn't handle non-finite values.
Results may differ from the reference program's by a relative error of at most 0.02.
Values may be sent and summed in bfloat16 or wider, within the bound.
No kernel may reach another device: no remote copies, remote signals or barrier semaphores. Data moves between devices by JAX's collectives and lax.ppermute only.
A program may use at most 192 MiB of HBM per device.

```python
import math
import jax
import jax.numpy as jnp
import numpy as np
from jax import lax

NP = 4
LEV = 128
HID = 384
SUB = 4
RIB = 16
EL_DEV = 128
FEAT = 512
ELEMS = 16384


def ribbon(key):
    column_total = ELEMS // RIB
    flipped = jax.random.randint(jax.random.fold_in(key, 101), (column_total,), 0, 2)
    marked = jax.random.randint(jax.random.fold_in(key, 102), (column_total, RIB), 0, 8) == 0
    marked = marked.at[0, 0].set(True).at[0, 1].set(False)
    return (flipped, marked)


def position(column, row_pos, flipped):
    column_total = ELEMS // RIB
    column = jnp.mod(column, column_total)
    row_pos = jnp.mod(row_pos, RIB)
    return column * RIB + jnp.where(flipped[column] == 1, RIB - 1 - row_pos, row_pos)


def located(flipped):
    positions = jnp.arange(ELEMS, dtype=jnp.int32)
    column = positions // RIB
    inside = positions % RIB
    row_pos = jnp.where(flipped[column] == 1, RIB - 1 - inside, inside)
    return (column, row_pos)


def draw_neighbours(key, part):
    flipped, marked = ribbon(key)
    column, row_pos = located(flipped)
    moves = [(1, 0), (-1, 0), (0, 1), (0, -1), (1, 1), (1, -1), (-1, 1), (-1, -1)]
    return jnp.stack([position(column + move_a, row_pos + move_b, flipped) for move_a, move_b in moves], axis=1).astype(jnp.int32)


def draw_valence(key, part):
    flipped, marked = ribbon(key)
    column, row_pos = located(flipped)
    column_total = ELEMS // RIB
    nodes = [(0, 0), (0, -1), (-1, 0), (-1, -1)]
    result = []
    for move_a, move_b in nodes:
        node_col = jnp.mod(column + move_a, column_total)
        node_row = jnp.mod(row_pos + move_b, RIB)
        result.append(jnp.where(marked[node_col, node_row], 3, 4))
    return jnp.stack(result, axis=1).astype(jnp.int32)


def draw_cost(key, part):
    key = jax.random.fold_in(key, 3)
    regions = ELEMS // EL_DEV
    hot_region = jax.random.randint(jax.random.fold_in(key, 11), (regions,), 0, 8) == 0
    drawn_level = jax.random.randint(jax.random.fold_in(key, 12), (regions,), 0, 3)
    regime = jnp.where(hot_region, 3, drawn_level).at[0].set(3)
    chance = jax.random.randint(jax.random.fold_in(key, 13), (ELEMS, NP * NP), 0, 4)
    chance = chance.at[0, 0].set(1).at[0, 1].set(0)
    region_of = jnp.arange(ELEMS, dtype=jnp.int32) // EL_DEV
    return (1 + regime[region_of][:, None] * (chance > 0).astype(jnp.int32)).astype(jnp.int32)


def block_levels(stream_key, extent, shards, least, top_value):
    def one(dim, blocks):
        steps = jax.random.uniform(jax.random.fold_in(jax.random.fold_in(stream_key, 6), dim), (blocks,), jnp.float32, least / len(shards), top_value / len(shards))
        return jnp.repeat(jnp.exp(steps), extent[dim] // blocks).reshape((-1,) + (1,) * (len(extent) - dim - 1))

    gain = one(*shards[0])
    for cut in shards[1:]:
        gain = gain * one(*cut)
    return gain


def gaussian(rng, dims, deviation, reach, pieces=(), kind=jnp.bfloat16):
    entries = jax.random.normal(rng, dims, jnp.float32) * deviation
    if len(pieces) > 0:
        entries = block_levels(rng, dims, pieces, -0.22, 0.18) * entries
    return jnp.clip(entries, min=-reach, max=reach).astype(kind)


def setup_inputs(seed: int = 0) -> dict:
    key_list = jax.random.split(jax.random.key(seed), 9)
    return {
        "state": gaussian(key_list[0], (ELEMS, NP * NP, FEAT), 1.0, 6.0, ((0, 128),), jnp.float32),
        "winds": gaussian(key_list[1], (2, ELEMS, NP * NP, LEV), 0.5, 3.0, ((1, 128),), jnp.float32),
        "neighbours": draw_neighbours(jax.random.fold_in(key_list[8], 71), 0),
        "valence": draw_valence(jax.random.fold_in(key_list[8], 71), 0),
        "cost": draw_cost(jax.random.fold_in(key_list[8], 71), 0),
        "w_in": gaussian(key_list[5], (FEAT, HID), (FEAT // 2) ** -0.5, 0.375),
        "w_mid": gaussian(key_list[6], (3, HID, HID), (HID // 2) ** -0.5, 0.4375),
        "w_out": gaussian(key_list[7], (HID, FEAT), (HID // 4) ** -0.5, 0.625),
    }


def lobatto_table():
    nodes = np.array([-1.0, -1.0 / np.sqrt(5.0), 1.0 / np.sqrt(5.0), 1.0])
    weights = np.array([1.0 / np.prod([nodes[outer] - nodes[inner] for inner in range(4) if inner != outer]) for outer in range(4)])
    deriv_table = np.zeros((4, 4))
    for outer in range(4):
        for inner in range(4):
            if inner != outer:
                deriv_table[outer, inner] = weights[inner] / weights[outer] / (nodes[outer] - nodes[inner])
        deriv_table[outer, outer] = -np.sum(deriv_table[outer])
    return deriv_table.astype(np.float32)

def advection(field, winds_a, winds_b, levels):
    element_count = field.shape[0]
    deriv_numpy = lobatto_table()
    order_np = deriv_numpy.shape[0]
    deriv_table = jnp.asarray(deriv_numpy)
    grid_field = field.reshape(element_count, order_np, order_np, -1, levels)
    wind_a = winds_a.reshape(element_count, order_np, order_np, 1, levels)
    wind_b = winds_b.reshape(element_count, order_np, order_np, 1, levels)
    along_a = sum((deriv_table[None, :, column, None, None, None] * grid_field[:, None, column] for column in range(order_np)))
    along_b = sum((deriv_table[None, None, :, column, None, None] * grid_field[:, :, None, column] for column in range(order_np)))
    return -(wind_a * along_a + wind_b * along_b)

def assemble(own_field, pick_points, valence):
    order_np = own_field.shape[1]
    last_index = order_np - 1
    span_list = list(range(order_np))
    summed = own_field
    summed = summed.at[:, last_index].add(pick_points(0, [(0, column) for column in span_list]))
    summed = summed.at[:, 0].add(pick_points(1, [(last_index, column) for column in span_list]))
    summed = summed.at[:, :, last_index].add(pick_points(2, [(column, 0) for column in span_list]))
    summed = summed.at[:, :, 0].add(pick_points(3, [(column, last_index) for column in span_list]))
    edge_counts = np.ones((order_np, order_np), np.float32)
    edge_counts[0] += 1.0
    edge_counts[last_index] += 1.0
    edge_counts[:, 0] += 1.0
    edge_counts[:, last_index] += 1.0
    copies = jnp.broadcast_to(jnp.asarray(edge_counts), (own_field.shape[0], order_np, order_np))
    corner_list = [((last_index, last_index), (0, 0)), ((last_index, 0), (0, last_index)), ((0, last_index), (last_index, 0)), ((0, 0), (last_index, last_index))]
    for corner_index in range(4):
        own_point, far_point = corner_list[corner_index]
        present = (valence[:, corner_index] == 4).astype(copies.dtype)
        corner_value = pick_points(4 + corner_index, [far_point])[:, 0]
        summed = summed.at[:, own_point[0], own_point[1]].add(present[:, None] * corner_value)
        copies = copies.at[:, own_point[0], own_point[1]].add(present)
    return summed / copies[..., None]

def network(inputs, w_in, w_mid, w_out):
    hidden = jax.nn.silu(jnp.dot(inputs, w_in, preferred_element_type=jnp.float32)).astype(jnp.bfloat16)
    for layer in range(w_mid.shape[0]):
        hidden = jax.nn.silu(jnp.dot(hidden, w_mid[layer], preferred_element_type=jnp.float32)).astype(jnp.bfloat16)
    return jnp.dot(hidden, w_out, preferred_element_type=jnp.float32)

def network_block(column_start, counts, w_in, w_mid, w_out):
    begin_state = column_start.astype(jnp.float32)
    columns_now = begin_state
    for substep in range(SUB):
        increment = network(columns_now.astype(jnp.bfloat16), w_in, w_mid, w_out)
        columns_now = jnp.where((counts > substep)[:, None], columns_now + increment, columns_now)
    return (columns_now - begin_state).astype(jnp.bfloat16)

def reference(state, winds, neighbours, valence, cost, w_in, w_mid, w_out):
    element_count, points, features = state.shape
    order_np = 4
    advect = advection(state, winds[0], winds[1], LEV).reshape(element_count, order_np, order_np, features)
    flat_field = advect.reshape(element_count * points, features)

    def pick_points(slot_index, points_list):
        offsets = jnp.asarray([first * order_np + second for first, second in points_list], dtype=jnp.int32)
        row_ids = neighbours[:, slot_index][:, None] * points + offsets[None, :]
        return flat_field[row_ids]
    dyn_tend = assemble(advect, pick_points, valence).reshape(element_count, points, features)
    column_start = state.reshape(-1, features).astype(jnp.bfloat16)
    counts = cost.reshape(-1)
    row_count = column_start.shape[0]
    block_rows = math.gcd(row_count, 4096)
    blocks_in = column_start.reshape(row_count // block_rows, block_rows, features)
    blocks_count = counts.reshape(row_count // block_rows, block_rows)
    results = lax.map(lambda paired: network_block(paired[0], paired[1], w_in, w_mid, w_out), (blocks_in, blocks_count))
    phys_tend = results.reshape(element_count, points, features)
    return (dyn_tend, phys_tend)
```

```python
import jax
import jax.numpy as jnp
import numpy as np
from jax import lax
from jax.experimental import pallas as pl
from jax.experimental.pallas import tpu as pltpu
from jax.sharding import PartitionSpec as P

RIB = 16
SWEEPS = 8
ALL = 16384
F32 = jnp.float32
BF16 = jnp.bfloat16


def lobatto_table():
    nodes = np.array([-1.0, -1.0 / np.sqrt(5.0), 1.0 / np.sqrt(5.0), 1.0])
    weights = np.array(
        [
            1.0 / np.prod([nodes[outer] - nodes[inner] for inner in range(4) if inner != outer])
            for outer in range(4)
        ]
    )
    deriv = np.zeros((4, 4))
    for outer in range(4):
        for inner in range(4):
            if inner != outer:
                deriv[outer, inner] = weights[inner] / weights[outer] / (nodes[outer] - nodes[inner])
        deriv[outer, outer] = -np.sum(deriv[outer])
    return deriv.astype(np.float32)


def constant_table():
    deriv = lobatto_table()
    sub = np.arange(8)
    half, along = sub // 4, sub % 4
    rows = []
    for t in range(2):
        i = 2 * t + half
        for source in (half, 1 - half, 2 + half, 3 - half):
            rows.append(-deriv[i, source])
    for shift in range(4):
        rows.append(-deriv[along, (along + shift) % 4])
    for t in range(2):
        first, second = (0, 3) if t == 0 else (4, 7)
        edge = np.ones(8)
        edge += (half == t) * 1.0
        edge += (along == 0) * 1.0
        edge += (along == 3) * 1.0
        for pattern in range(4):
            present = np.zeros(8)
            present[first] = pattern // 2
            present[second] = pattern % 2
            rows.append(1.0 / (edge + present))
            rows.append(present / (edge + present))
    table = np.stack(rows).astype(np.float32)
    return np.ascontiguousarray(np.broadcast_to(table[:, :, None], table.shape + (128,)))


TABLE = constant_table()
A_AT, B_AT, W_AT = 0, 8, 12


def dot(a, b):
    return jnp.dot(a, b, preferred_element_type=F32)


def silu_half(h):
    return (h + h * jnp.tanh(h)).astype(BF16)


def sublanes():
    return lax.broadcasted_iota(jnp.int32, (8, 128), 0)


def element_advect(load, wind, table, halves, emit):
    sub = sublanes()
    along = sub % 4
    for v in range(4):
        low, high = load(0, v), load(1, v)
        pieces = (low, pltpu.roll(low, 4, 0), high, pltpu.roll(high, 4, 0))
        for t in halves:
            own = (low, high)[t]
            da = pieces[0] * table[A_AT + 4 * t]
            for k in range(1, 4):
                da = da + pieces[k] * table[A_AT + 4 * t + k]
            db = own * table[B_AT]
            for shift in range(1, 4):
                turned = jnp.where(
                    along < 4 - shift, pltpu.roll(own, 8 - shift, 0), pltpu.roll(own, 4 - shift, 0)
                )
                db = db + turned * table[B_AT + shift]
            emit(t, v, wind(0, t) * da + wind(1, t) * db)


def edge_kernel(first, last, wind_first, wind_last, table, low_out, high_out):
    def run(e, _):
        for field, wind, out, t in (
            (first, wind_first, low_out, 0),
            (last, wind_last, high_out, 1),
        ):

            def emit(t, v, value, out=out):
                at = 4 * t
                out[e, :, 128 * v : 128 * (v + 1)] = value[at : at + 4]

            element_advect(
                lambda t, v, field=field: field[e, 8 * t : 8 * t + 8, 128 * v : 128 * (v + 1)],
                lambda d, t, wind=wind: wind[d, e, 8 * t : 8 * t + 8, :],
                table,
                (t,),
                emit,
            )
        return 0

    lax.fori_loop(0, RIB, run, 0, unroll=4)


def main_kernel(
    base,
    neighbours,
    valence,
    cost,
    table,
    w_in,
    w_mid,
    w_out,
    state_hbm,
    winds_hbm,
    dyn_hbm,
    phys_hbm,
    state,
    winds,
    adv,
    dyn,
    phys,
    wi,
    wm,
    in_sem,
    out_sem,
):
    def state_copy(s):
        return pltpu.make_async_copy(
            state_hbm.at[pl.ds(s * RIB, RIB)], state.at[pl.ds(s * RIB, RIB)], in_sem.at[0, s]
        )

    def winds_copy(d, s):
        return pltpu.make_async_copy(
            winds_hbm.at[d, pl.ds(s * RIB, RIB)],
            winds.at[d, pl.ds(s * RIB, RIB)],
            in_sem.at[1 + d, s],
        )

    for s in range(SWEEPS):
        state_copy(s).start()
        winds_copy(0, s).start()
        winds_copy(1, s).start()

    def arrive(s):
        state_copy(s).wait()
        winds_copy(0, s).wait()
        winds_copy(1, s).wait()

    for v in range(4):
        adv[v, : 16 * RIB, :] = jnp.zeros((16 * RIB, 128), F32)
        adv[v, 16 * RIB * (SWEEPS + 1) : 16 * RIB * (SWEEPS + 2), :] = jnp.zeros((16 * RIB, 128), F32)
    wi[...] = w_in[...] * 0.5
    for k in range(3):
        wm[k] = w_mid[k] * 0.5
    wm[3] = (dot(w_out[...], w_in[...]) * 0.5).astype(BF16)

    def advect(e, to):
        def emit(t, v, value):
            adv[v, pl.ds(pl.multiple_of(to * 16 + 8 * t, 8), 8), :] = value

        element_advect(
            lambda t, v: state[e, 8 * t : 8 * t + 8, 128 * v : 128 * (v + 1)],
            lambda d, t: winds[d, e, 8 * t : 8 * t + 8, :],
            table,
            (0, 1),
            emit,
        )

    def assemble(e):
        sub = sublanes()
        along = sub % 4
        at = [(((neighbours[e, c] - base[0] + RIB) & (ALL - 1)) * 16) for c in range(8)]
        four = [jnp.where(valence[e, c] == 4, 1, 0) for c in range(4)]
        pattern = (four[3] * 2 + four[2], four[1] * 2 + four[0])
        own_at = pl.multiple_of((e + RIB) * 16, 16)
        for t in range(2):
            weight = table[W_AT + 8 * t + 2 * pattern[t]]
            corner = table[W_AT + 8 * t + 2 * pattern[t] + 1]
            for v in range(4):

                def rows(start):
                    return adv[v, pl.ds(start, 8), :]

                if t == 0:
                    across = jnp.where(sub < 4, rows(at[1] + 12), 0.0)
                    diagonal = jnp.where(sub == 0, rows(at[7] + 15), rows(at[6] + 9))
                else:
                    across = jnp.where(sub >= 4, rows(at[0] - 4), 0.0)
                    diagonal = jnp.where(sub == 4, rows(at[5] - 1), rows(at[4] - 7))
                beside = jnp.where(
                    along == 3,
                    rows(at[2] + 8 * t - 3),
                    jnp.where(along == 0, rows(at[3] + 8 * t + 3), 0.0),
                )
                own = adv[v, pl.ds(own_at + 8 * t, 8), :]
                dyn[e, 8 * t : 8 * t + 8, 128 * v : 128 * (v + 1)] = (
                    own + across + beside
                ) * weight + diagonal * corner

    def network(first_element, costs):
        x = state[pl.ds(first_element, RIB)].reshape(16 * RIB, 512).astype(BF16)
        a = dot(x, wi[...])
        yield
        total = None
        for s in range(4):
            h = silu_half(a)
            for k in range(3):
                h = dot(h, wm[k])
                yield
                h = silu_half(h)
            wide = h.astype(F32)
            if s == 0:
                total = wide
            else:
                active = costs > s
                total = total + jnp.concatenate(
                    [
                        jnp.where(active, wide[:, 128 * v : 128 * (v + 1)], 0.0)
                        for v in range(3)
                    ],
                    1,
                )
            if s < 3:
                a = a + dot(h, wm[3])
                yield
        tend = dot(total.astype(BF16), w_out[...])
        phys[pl.ds(first_element, RIB)] = tend.astype(BF16).reshape(RIB, 16, 512)

    def column_costs(first_element):
        block = cost[pl.ds(first_element, RIB), :].astype(F32)
        spread = jnp.broadcast_to(block[:, None, :], (RIB, 16, 16))
        point = lax.broadcasted_iota(jnp.int32, (RIB, 16, 16), 1)
        lane = lax.broadcasted_iota(jnp.int32, (RIB, 16, 16), 2)
        spread = jnp.where(point == lane, spread, 0.0).reshape(16 * RIB, 16)
        return dot(spread.astype(BF16), jnp.ones((16, 128), BF16))

    def dyn_copy(t):
        return pltpu.make_async_copy(
            dyn.at[pl.ds(t * 32, 32)], dyn_hbm.at[pl.ds(t * 32, 32)], out_sem.at[0, t]
        )

    def phys_copy(t):
        return pltpu.make_async_copy(
            phys.at[pl.ds(t * 32, 32)], phys_hbm.at[pl.ds(t * 32, 32)], out_sem.at[1, t]
        )

    arrive(0)

    def first_advect(e, _):
        advect(e, e + RIB)
        return 0

    lax.fori_loop(0, RIB, first_advect, 0, unroll=4)

    def step(t, _):
        arrive(2 * t + 1)

        @pl.when(t < 3)
        def _():
            arrive(2 * t + 2)

        def fill():
            for e in range(32):
                number = t * 32 + RIB + e
                if e < RIB:
                    advect(number, number + RIB)
                else:
                    advect(
                        jnp.minimum(number, RIB * SWEEPS - RIB + e - RIB),
                        jnp.where(t == 3, RIB * (SWEEPS + 2) + e - RIB, number + RIB),
                    )
                if e % 4 == 3:
                    yield
            for e in range(32):
                assemble(t * 32 + e)
                if e % 4 == 3:
                    yield

        chains = [
            network(t * 32 + c * RIB, column_costs(t * 32 + c * RIB)) for c in range(2)
        ]
        live = chains + [fill()]
        while live:
            later = []
            for part in live:
                try:
                    next(part)
                    later.append(part)
                except StopIteration:
                    pass
            live = later
        dyn_copy(t).start()
        phys_copy(t).start()
        return 0

    lax.fori_loop(0, 4, step, 0)
    for t in range(4):
        dyn_copy(t).wait()
        phys_copy(t).wait()


def halo_kernel(
    base, neighbours, valence, table, before, after, dyn_in, dyn_hbm, low, high, sem
):
    last = RIB * (SWEEPS - 1)
    parts = (
        (low, dyn_hbm.at[pl.ds(0, RIB), pl.ds(0, 8)], 0),
        (high, dyn_hbm.at[pl.ds(last, RIB), pl.ds(8, 8)], 1),
    )
    loads = [pltpu.make_async_copy(far, near, sem.at[k]) for near, far, k in parts]
    stores = [pltpu.make_async_copy(near, far, sem.at[2 + k]) for near, far, k in parts]
    for copy in loads:
        copy.start()
    for copy in loads:
        copy.wait()
    sub = lax.broadcasted_iota(jnp.int32, (4, 512), 0)

    def wide(entry):
        return jnp.concatenate([entry] * 4, 1)

    def run(e, _):
        for near, t, halo, first in ((low, 0, before, 0), (high, 1, after, last)):
            own = e + first
            slots = (1, 7, 6) if t == 0 else (0, 5, 4)
            origin = base[0] + (RIB * SWEEPS if t else -RIB)
            at = [(neighbours[own, c] - origin) & (ALL - 1) for c in slots]
            four = [jnp.where(valence[own, c] == 4, 1, 0) for c in range(4)]
            pattern = (four[3] * 2 + four[2], four[1] * 2 + four[0])[t]
            weight = table[W_AT + 8 * t + 2 * pattern, 4 * t : 4 * t + 4, :]
            corner = table[W_AT + 8 * t + 2 * pattern + 1, 4 * t : 4 * t + 4, :]
            diagonal = jnp.where(sub == 0, halo[at[1], 3:4, :], halo[at[2], 0:1, :])
            near[e, 4 * t : 4 * t + 4, :] = (
                near[e, 4 * t : 4 * t + 4, :]
                + halo[at[0]] * wide(weight)
                + diagonal * wide(corner)
            )
        return 0

    lax.fori_loop(0, RIB, run, 0, unroll=4)
    for copy in stores:
        copy.start()
    for copy in stores:
        copy.wait()


def body(state, winds, neighbours, valence, cost, w_in, w_mid, w_out):
    vmem = pl.BlockSpec(memory_space=pltpu.VMEM)
    smem = pl.BlockSpec(memory_space=pltpu.SMEM)
    anywhere = pl.BlockSpec(memory_space=pl.ANY)
    devices = lax.axis_size("dev")
    base = (lax.axis_index("dev") * (RIB * SWEEPS)).astype(jnp.int32).reshape(1)
    table = jnp.asarray(TABLE)

    def sweep_of(which):
        return pl.BlockSpec((RIB, 16, 512), lambda i: (which, 0, 0))

    def winds_of(which):
        return pl.BlockSpec((2, RIB, 16, 128), lambda i: (0, which, 0, 0))

    edge = jax.ShapeDtypeStruct((RIB, 4, 512), F32)
    edge_spec = pl.BlockSpec((RIB, 4, 512), lambda i: (0, 0, 0))
    low, high = pl.pallas_call(
        edge_kernel,
        grid=(1,),
        out_shape=(edge, edge),
        in_specs=[
            sweep_of(0),
            sweep_of(SWEEPS - 1),
            winds_of(0),
            winds_of(SWEEPS - 1),
            pl.BlockSpec(TABLE.shape, lambda i: (0, 0, 0)),
        ],
        out_specs=(edge_spec, edge_spec),
        cost_estimate=pl.CostEstimate(
            flops=10_000_000, bytes_accessed=2_000_000, transcendentals=0
        ),
    )(state, state, winds, winds, table)
    forward = [(i, (i + 1) % devices) for i in range(devices)]
    backward = [(target, source) for source, target in forward]
    before = lax.ppermute(high, "dev", forward)
    after = lax.ppermute(low, "dev", backward)

    dyn, phys = pl.pallas_call(
        main_kernel,
        out_shape=(
            jax.ShapeDtypeStruct(state.shape, F32),
            jax.ShapeDtypeStruct(state.shape, BF16),
        ),
        in_specs=[smem, smem, smem, vmem, vmem, vmem, vmem, vmem, anywhere, anywhere],
        out_specs=(anywhere, anywhere),
        scratch_shapes=[
            pltpu.VMEM((RIB * SWEEPS, 16, 512), F32),
            pltpu.VMEM((2, RIB * SWEEPS, 16, 128), F32),
            pltpu.VMEM((4, (SWEEPS + 3) * RIB * 16, 128), F32),
            pltpu.VMEM((RIB * SWEEPS, 16, 512), F32),
            pltpu.VMEM((RIB * SWEEPS, 16, 512), BF16),
            pltpu.VMEM((512, 384), BF16),
            pltpu.VMEM((4, 384, 384), BF16),
            pltpu.SemaphoreType.DMA((3, SWEEPS)),
            pltpu.SemaphoreType.DMA((2, 4)),
        ],
        compiler_params=pltpu.CompilerParams(vmem_limit_bytes=44 * 2**20),
        cost_estimate=pl.CostEstimate(
            flops=12_000_000_000, bytes_accessed=14_000_000, transcendentals=10_000_000
        ),
    )(base, neighbours, valence, cost, table, w_in, w_mid, w_out, state, winds)

    dyn = pl.pallas_call(
        halo_kernel,
        out_shape=jax.ShapeDtypeStruct(state.shape, F32),
        in_specs=[smem, smem, smem, vmem, vmem, vmem, anywhere],
        out_specs=anywhere,
        scratch_shapes=[
            pltpu.VMEM((RIB, 8, 512), F32),
            pltpu.VMEM((RIB, 8, 512), F32),
            pltpu.SemaphoreType.DMA((4,)),
        ],
        input_output_aliases={6: 0},
        cost_estimate=pl.CostEstimate(
            flops=1_000_000, bytes_accessed=2_000_000, transcendentals=0
        ),
    )(base, neighbours, valence, table, before, after, dyn)
    return dyn, phys


def solution(mesh):
    return jax.shard_map(
        body,
        mesh=mesh,
        in_specs=(
            P("dev", None, None),
            P(None, "dev", None, None),
            P("dev", None),
            P("dev", None),
            P("dev", None),
            P(),
            P(),
            P(),
        ),
        out_specs=(P("dev", None, None), P("dev", None, None)),
        check_vma=False,
    )
```

```python
import functools

import jax
import jax.numpy as jnp
import numpy as np
from jax import lax
from jax.experimental import pallas as pl
from jax.experimental.pallas import tpu as pltpu
from jax.sharding import PartitionSpec as P

RIB = 16
SWEEPS = 8
STEPS = 4
ALL = 16384
F32 = jnp.float32
BF16 = jnp.bfloat16


def lobatto_table():
    nodes = np.array([-1.0, -1.0 / np.sqrt(5.0), 1.0 / np.sqrt(5.0), 1.0])
    weights = np.array(
        [
            1.0 / np.prod([nodes[outer] - nodes[inner] for inner in range(4) if inner != outer])
            for outer in range(4)
        ]
    )
    deriv = np.zeros((4, 4))
    for outer in range(4):
        for inner in range(4):
            if inner != outer:
                deriv[outer, inner] = weights[inner] / weights[outer] / (nodes[outer] - nodes[inner])
        deriv[outer, outer] = -np.sum(deriv[outer])
    return deriv.astype(np.float32)


def constant_table():
    deriv = lobatto_table()
    sub = np.arange(8)
    half, along = sub // 4, sub % 4
    rows = []
    for t in range(2):
        i = 2 * t + half
        for source in (half, 1 - half, 2 + half, 3 - half):
            rows.append(-deriv[i, source])
    for shift in range(4):
        rows.append(-deriv[along, (along + shift) % 4])
    for t in range(2):
        first, second = (0, 3) if t == 0 else (4, 7)
        edge = np.ones(8)
        edge += (half == t) * 1.0
        edge += (along == 0) * 1.0
        edge += (along == 3) * 1.0
        for pattern in range(4):
            present = np.zeros(8)
            present[first] = pattern // 2
            present[second] = pattern % 2
            rows.append(1.0 / (edge + present))
            rows.append(present / (edge + present))
    table = np.stack(rows).astype(np.float32)
    return np.ascontiguousarray(np.broadcast_to(table[:, :, None], table.shape + (128,)))


TABLE = constant_table()
A_AT, B_AT, W_AT = 0, 8, 12
LAYERS = 16


def dot(a, b):
    return jnp.dot(a, b, preferred_element_type=F32)


def silu_half(h):
    h = h.astype(BF16)
    return h + h * jnp.tanh(h)


def sublanes():
    return lax.broadcasted_iota(jnp.int32, (8, 128), 0)


def turned(tile, pattern):
    return jnp.take_along_axis(tile, pattern, axis=0, mode="promise_in_bounds")


def element_advect(load, wind, table, halves, emit):
    sub = sublanes()
    swap = sub ^ 4
    shifts = [(sub & 4) | ((sub + shift) & 3) for shift in range(4)]
    for v in range(4):
        low, high = load(0, v), load(1, v)
        pieces = (low, turned(low, swap), high, turned(high, swap))
        for t in halves:
            own = (low, high)[t]
            da = pieces[0] * table[A_AT + 4 * t]
            for k in range(1, 4):
                da = da + pieces[k] * table[A_AT + 4 * t + k]
            db = own * table[B_AT]
            for shift in range(1, 4):
                db = db + turned(own, shifts[shift]) * table[B_AT + shift]
            emit(t, v, wind(0, t) * da + wind(1, t) * db)


def half_split(base):
    return 2


def main_kernel(opening, *refs):
    if opening:
        (base, neighbours, valence, cost, table, w_in, w_mid, w_out, state_hbm, winds_hbm,
         dyn_hbm, phys_hbm, edge_low, edge_high, part, plan_out, wi, wm, wo,
         state, winds, adv, dyn, phys, plan, plan_sem, w_sem, in_sem, out_sem) = refs
    else:
        (base, plan, cost, table, wi, wm, wo, state_hbm, winds_hbm, _, _,
         dyn_hbm, phys_hbm, part,
         state, winds, adv, dyn, phys, in_sem, out_sem) = refs
    middle = half_split(base[0])
    first_step, last_step = (0, middle) if opening else (middle, STEPS)

    def copies(s):
        at = pl.ds(s * RIB, RIB)
        return (
            pltpu.make_async_copy(state_hbm.at[at], state.at[at], in_sem.at[0, s]),
            pltpu.make_async_copy(winds_hbm.at[0, at], winds.at[0, at], in_sem.at[1, s]),
            pltpu.make_async_copy(winds_hbm.at[1, at], winds.at[1, at], in_sem.at[2, s]),
        )

    def fetch(s):
        for copy in copies(s):
            copy.start()

    def arrive(s):
        for copy in copies(s):
            copy.wait()

    def each(start, stop, act):
        def one(s, _):
            act(s)
            return 0

        lax.fori_loop(start, stop, one, 0)

    if opening:
        fetch(0)
        fetch(SWEEPS - 1)
        loads = [
            pltpu.make_async_copy(w_in, wi, w_sem.at[0]),
            pltpu.make_async_copy(w_mid, wm.at[pl.ds(0, 3)], w_sem.at[1]),
            pltpu.make_async_copy(w_out, wo, w_sem.at[2]),
        ]
        for copy in loads:
            copy.start()
        each(1, 2 * last_step + 1, fetch)
        rows = ((neighbours[...] - base[0] + RIB) & (ALL - 1)) * 16
        plan_out[0:8, :] = rows
        corner = valence[...] - 3
        plan_out[8:9, :] = corner[3:4] * 4 + corner[2:3] * 2 + W_AT
        plan_out[9:10, :] = corner[1:2] * 4 + corner[0:1] * 2 + W_AT + 8
        plan_out[10:16, :] = jnp.zeros((6, 128), jnp.int32)
        send_plan = pltpu.make_async_copy(plan_out, plan, plan_sem)
        send_plan.start()
    else:
        each(2 * first_step - 1, SWEEPS, fetch)

    for v in range(4):
        adv[v, : 16 * RIB, :] = jnp.zeros((16 * RIB, 128), F32)
        adv[v, 16 * RIB * (SWEEPS + 1) : 16 * RIB * (SWEEPS + 2), :] = jnp.zeros(
            (16 * RIB, 128), F32
        )
    costs = lax.dot_general(
        cost[...].astype(BF16),
        (
            lax.broadcasted_iota(jnp.int32, (16, 16), 0)
            == lax.broadcasted_iota(jnp.int32, (16, 16), 1)
        ).astype(BF16),
        (((0,), (0,)), ((), ())),
        preferred_element_type=F32,
    )

    def advect(e, to, halves=(0, 1), emit=None):
        def keep(t, v, value):
            adv[v, pl.ds(pl.multiple_of(to * 16 + 8 * t, 8), 8), :] = value
            if emit is not None:
                emit(t, v, value)

        element_advect(
            lambda t, v: state[e, 8 * t : 8 * t + 8, 128 * v : 128 * (v + 1)],
            lambda d, t: winds[d, e, 8 * t : 8 * t + 8, :],
            table,
            halves,
            keep,
        )

    def assemble(e, half=None):
        sub = sublanes()
        along = sub % 4
        at = [plan[c, e] for c in range(8)]
        own_at = pl.multiple_of((e + RIB) * 16, 16)
        for t in range(2):
            entry = plan[8 + t, e]
            weight = table[entry]
            corner = table[entry + 1]
            for v in range(4):

                def rows(start):
                    return adv[v, pl.ds(start, 8), :]

                if t == 0:
                    across = jnp.where(sub < 4, rows(at[1] + 12), 0.0)
                    diagonal = jnp.where(sub == 0, rows(at[7] + 15), rows(at[6] + 9))
                else:
                    across = jnp.where(sub >= 4, rows(at[0] - 4), 0.0)
                    diagonal = jnp.where(sub == 4, rows(at[5] - 1), rows(at[4] - 7))
                beside = jnp.where(
                    along == 3,
                    rows(at[2] + 8 * t - 3),
                    jnp.where(along == 0, rows(at[3] + 8 * t + 3), 0.0),
                )
                own = adv[v, pl.ds(own_at + 8 * t, 8), :]
                dyn[e, 8 * t : 8 * t + 8, 128 * v : 128 * (v + 1)] = (
                    own + across + beside
                ) * weight + diagonal * corner

    def network(first_element, counts):
        x = state[pl.ds(first_element, RIB)].reshape(16 * RIB, 512).astype(BF16)
        a = dot(x, wi[...])
        yield a[:8, :128]
        total = None
        for s in range(4):
            h = silu_half(a)
            for k in range(3):
                pre = dot(h, wm[k])
                yield pre[:8, :128]
                h = silu_half(pre)
            wide = h.astype(F32)
            if s == 0:
                total = wide
            else:
                active = counts > s
                total = total + jnp.concatenate(
                    [
                        jnp.where(active, wide[:, 128 * v : 128 * (v + 1)], 0.0)
                        for v in range(3)
                    ],
                    1,
                )
            if s < 3:
                a = a + dot(h, wm[3])
                yield a[:8, :128]
        tend = dot(total.astype(BF16), wo[...])
        phys[pl.ds(first_element, RIB)] = tend.astype(BF16).reshape(RIB, 16, 512)

    def column_counts(first_element):
        block = costs_ref(first_element)
        spread = jnp.broadcast_to(block[:, None, :], (RIB, 16, 16))
        point = lax.broadcasted_iota(jnp.int32, (RIB, 16, 16), 1)
        lane = lax.broadcasted_iota(jnp.int32, (RIB, 16, 16), 2)
        spread = jnp.where(point == lane, spread, 0.0).reshape(16 * RIB, 16)
        return dot(spread.astype(BF16), jnp.ones((16, 128), BF16))

    for s in range(SWEEPS):
        winds[0, RIB * SWEEPS + s, :, 0:16] = costs[s * RIB : (s + 1) * RIB]

    def costs_ref(first_element):
        return winds[0, RIB * SWEEPS + first_element // RIB, :, 0:16]

    def results(t):
        at = pl.ds(t * 2 * RIB, 2 * RIB)
        return (
            pltpu.make_async_copy(dyn.at[at], dyn_hbm.at[at], out_sem.at[0, t]),
            pltpu.make_async_copy(phys.at[at], phys_hbm.at[at], out_sem.at[1, t]),
        )

    if opening:
        send_plan.wait()
        arrive(0)
        arrive(SWEEPS - 1)
        sub = sublanes()

        def edges(e, _):
            def low(t, v, value):
                if t == 0:
                    edge_low[e, :, 128 * v : 128 * (v + 1)] = jnp.where(
                        sub >= 4, turned(value, sub ^ 4), 0.0
                    )

            def high(t, v, value):
                edge_high[e, :, 128 * v : 128 * (v + 1)] = jnp.where(
                    sub < 4, turned(value, sub ^ 4), 0.0
                )

            advect(e, e + RIB, emit=low)
            advect(e + RIB * (SWEEPS - 1), e + RIB * SWEEPS, (1,), high)
            return 0

        lax.fori_loop(0, RIB, edges, 0, unroll=4)
        for copy in loads:
            copy.wait()
        wm[3] = (dot(wo[...], wi[...]) * 0.5).astype(BF16)
        wi[...] = wi[...] * 0.5
        for k in range(3):
            wm[k] = wm[k] * 0.5
    else:
        arrive(2 * first_step - 1)
        arrive(2 * first_step)

        def before(e, _):
            number = e + (2 * first_step - 1) * RIB
            advect(number, number + RIB)
            return 0

        lax.fori_loop(0, 2 * RIB, before, 0, unroll=4)

    def step(t, _):
        arrive(2 * t + 1)

        @pl.when(t < STEPS - 1)
        def _():
            arrive(2 * t + 2)

        def tasks():
            for e in range(32):
                number = t * 32 + RIB + e
                if e < RIB:
                    advect(number, number + RIB)
                else:
                    advect(
                        jnp.minimum(number, RIB * SWEEPS - RIB + e - RIB),
                        jnp.where(
                            t == STEPS - 1, RIB * (SWEEPS + 2) + e - RIB, number + RIB
                        ),
                    )
                    assemble(t * 32 + e - RIB)
                yield
            for e in range(RIB):
                assemble(t * 32 + RIB + e)
                yield

        chains = [
            network(t * 32 + c * RIB, column_counts(t * 32 + c * RIB)) for c in range(2)
        ]
        left = tasks()
        share = 0.0
        for _ in range(LAYERS):
            for chain in chains:
                pace = next(chain)
                state[RIB * SWEEPS, 0:8, 0:128] = pace
                adv[0, 16 * RIB * (SWEEPS + 3) :, :] = pace
                share += 48 / (2 * LAYERS)
                while share >= 1.0:
                    next(left)
                    share -= 1.0
        for rest in (*chains, left):
            for _ in rest:
                pass
        for copy in results(t):
            copy.start()
        return 0

    lax.fori_loop(first_step, last_step, step, 0)
    t = 0 if opening else 1
    part[...] = dyn[pl.ds(t * RIB * (SWEEPS - 1), RIB), 8 * t : 8 * t + 8, :]
    each(first_step, last_step, lambda s: [copy.wait() for copy in results(s)])


def halo_kernel(
    base, plan, table, before, after, part_low, part_high, dyn_in, dyn_hbm, low, high, sem
):
    last = RIB * (SWEEPS - 1)
    sub = sublanes()
    for near, part, t, halo, first in (
        (low, part_low, 0, before, 0),
        (high, part_high, 1, after, last),
    ):
        origin = RIB * (SWEEPS + 1) if t else 0
        slots = (0, 5, 4) if t else (1, 7, 6)
        left, right = 4 * t, 4 * t + 3

        def run(e, _):
            own = e + first
            at = [(plan[c, own] >> 4) - origin for c in slots]
            entry = plan[8 + t, own]
            for v in range(4):
                lanes = slice(128 * v, 128 * (v + 1))
                diagonal = jnp.where(
                    sub == left,
                    pltpu.roll(halo[at[1], :, lanes], 5, 0),
                    pltpu.roll(halo[at[2], :, lanes], 3, 0),
                )
                near[e, :, lanes] = (
                    part[e, :, lanes]
                    + halo[at[0], :, lanes] * table[entry]
                    + diagonal * table[entry + 1]
                )
            return 0

        lax.fori_loop(0, RIB, run, 0, unroll=8)
        pltpu.make_async_copy(
            near, dyn_hbm.at[pl.ds(first, RIB), pl.ds(8 * t, 8)], sem.at[t]
        ).start()
    for near, t, first in ((low, 0, 0), (high, 1, last)):
        pltpu.make_async_copy(
            near, dyn_hbm.at[pl.ds(first, RIB), pl.ds(8 * t, 8)], sem.at[t]
        ).wait()


def body(state, winds, neighbours, valence, cost, w_in, w_mid, w_out):
    vmem = pl.BlockSpec(memory_space=pltpu.VMEM)
    smem = pl.BlockSpec(memory_space=pltpu.SMEM)
    hbm = pl.BlockSpec(memory_space=pltpu.HBM)
    devices = lax.axis_size("dev")
    base = (lax.axis_index("dev") * (RIB * SWEEPS)).astype(jnp.int32).reshape(1)
    table = jnp.asarray(TABLE)
    dyn = jax.ShapeDtypeStruct(state.shape, F32)
    phys = jax.ShapeDtypeStruct(state.shape, BF16)
    edge = jax.ShapeDtypeStruct((RIB, 8, 512), F32)
    scratch = [
        pltpu.VMEM((RIB * SWEEPS + 1, 16, 512), F32),
        pltpu.VMEM((2, RIB * SWEEPS + SWEEPS, 16, 128), F32),
        pltpu.VMEM((4, (SWEEPS + 3) * RIB * 16 + 8, 128), F32),
        pltpu.VMEM((RIB * SWEEPS, 16, 512), F32),
        pltpu.VMEM((RIB * SWEEPS, 16, 512), BF16),
    ]
    semaphores = [pltpu.SemaphoreType.DMA((3, SWEEPS)), pltpu.SemaphoreType.DMA((2, STEPS))]
    params = dict(
        compiler_params=pltpu.CompilerParams(vmem_limit_bytes=40 * 2**20),
        cost_estimate=pl.CostEstimate(
            flops=6_000_000_000, bytes_accessed=7_000_000, transcendentals=5_000_000
        ),
    )
    costs = cost.T
    dyn, phys, low, high, part_low, plan, wi, wm, wo = pl.pallas_call(
        functools.partial(main_kernel, True),
        out_shape=(
            dyn,
            phys,
            edge,
            edge,
            edge,
            jax.ShapeDtypeStruct((16, RIB * SWEEPS), jnp.int32),
            jax.ShapeDtypeStruct(w_in.shape, BF16),
            jax.ShapeDtypeStruct((4, 384, 384), BF16),
            jax.ShapeDtypeStruct(w_out.shape, BF16),
        ),
        in_specs=[smem] + [vmem] * 4 + [hbm] * 5,
        out_specs=[hbm] * 2 + [vmem] * 7,
        scratch_shapes=scratch
        + [
            pltpu.SMEM((16, RIB * SWEEPS), jnp.int32),
            pltpu.SemaphoreType.DMA(()),
            pltpu.SemaphoreType.DMA((3,)),
        ]
        + semaphores,
        **params,
    )(base, neighbours.T, valence.T, costs, table, w_in, w_mid, w_out, state, winds)
    forward = [(i, (i + 1) % devices) for i in range(devices)]
    backward = [(target, source) for source, target in forward]
    before = lax.ppermute(high, "dev", forward)
    after = lax.ppermute(low, "dev", backward)

    dyn, phys, part_high = pl.pallas_call(
        functools.partial(main_kernel, False),
        out_shape=(
            jax.ShapeDtypeStruct(state.shape, F32),
            jax.ShapeDtypeStruct(state.shape, BF16),
            edge,
        ),
        in_specs=[smem] * 2 + [vmem] * 5 + [hbm] * 4,
        out_specs=[hbm] * 2 + [vmem],
        scratch_shapes=scratch + semaphores,
        input_output_aliases={9: 0, 10: 1},
        **params,
    )(base, plan, costs, table, wi, wm, wo, state, winds, dyn, phys)

    dyn = pl.pallas_call(
        halo_kernel,
        out_shape=jax.ShapeDtypeStruct(state.shape, F32),
        in_specs=[smem] * 2 + [vmem] * 5 + [hbm],
        out_specs=hbm,
        scratch_shapes=[
            pltpu.VMEM((RIB, 8, 512), F32),
            pltpu.VMEM((RIB, 8, 512), F32),
            pltpu.SemaphoreType.DMA((2,)),
        ],
        input_output_aliases={7: 0},
        cost_estimate=pl.CostEstimate(
            flops=1_000_000, bytes_accessed=2_000_000, transcendentals=0
        ),
    )(base, plan, table, before, after, part_low, part_high, dyn)
    return dyn, phys


def solution(mesh):
    return jax.shard_map(
        body,
        mesh=mesh,
        in_specs=(
            P("dev", None, None),
            P(None, "dev", None, None),
            P("dev", None),
            P("dev", None),
            P("dev", None),
            P(),
            P(),
            P(),
        ),
        out_specs=(P("dev", None, None), P("dev", None, None)),
        check_vma=False,
    )
```

```python
import functools

import jax
import jax.numpy as jnp
import numpy as np
from jax import lax
from jax.experimental import pallas as pl
from jax.experimental.pallas import tpu as pltpu
from jax.sharding import PartitionSpec as P

RIB = 16
SUB = 4
SWEEPS = 8
STEPS = 4
ALL = 16384
F32 = jnp.float32
BF16 = jnp.bfloat16


def lobatto_table():
    nodes = np.array([-1.0, -1.0 / np.sqrt(5.0), 1.0 / np.sqrt(5.0), 1.0])
    weights = np.array(
        [
            1.0 / np.prod([nodes[outer] - nodes[inner] for inner in range(4) if inner != outer])
            for outer in range(4)
        ]
    )
    deriv = np.zeros((4, 4))
    for outer in range(4):
        for inner in range(4):
            if inner != outer:
                deriv[outer, inner] = weights[inner] / weights[outer] / (nodes[outer] - nodes[inner])
        deriv[outer, outer] = -np.sum(deriv[outer])
    return deriv.astype(np.float32)


def constant_table():
    deriv = lobatto_table()
    sub = np.arange(8)
    half, along = sub // 4, sub % 4
    rows = []
    for t in range(2):
        i = 2 * t + half
        for source in (half, 1 - half, 2 + half, 3 - half):
            rows.append(-deriv[i, source])
    for shift in range(4):
        rows.append(-deriv[along, (along + shift) % 4])
    for t in range(2):
        first, second = (0, 3) if t == 0 else (4, 7)
        edge = np.ones(8)
        edge += (half == t) * 1.0
        edge += (along == 0) * 1.0
        edge += (along == 3) * 1.0
        for pattern in range(4):
            present = np.zeros(8)
            present[first] = pattern // 2
            present[second] = pattern % 2
            rows.append(1.0 / (edge + present))
            rows.append(present / (edge + present))
    table = np.stack(rows).astype(np.float32)
    return np.ascontiguousarray(np.broadcast_to(table[:, :, None], table.shape + (128,)))


TABLE = constant_table()
A_AT, B_AT, W_AT = 0, 8, 12


def dot(a, b):
    return jnp.dot(a, b, preferred_element_type=F32)


def silu_half(h):
    h = h.astype(BF16)
    return h + h * jnp.tanh(h)


def sublanes():
    return lax.broadcasted_iota(jnp.int32, (8, 128), 0)


def turned(tile, pattern):
    return jnp.take_along_axis(tile, pattern, axis=0, mode="promise_in_bounds")


def element_advect(load, wind, table, halves, emit):
    sub = sublanes()
    swap = sub ^ 4
    shifts = [(sub & 4) | ((sub + shift) & 3) for shift in range(4)]
    for v in range(4):
        low, high = load(0, v), load(1, v)
        pieces = (low, turned(low, swap), high, turned(high, swap))
        for t in halves:
            own = (low, high)[t]
            da = pieces[0] * table[A_AT + 4 * t]
            for k in range(1, 4):
                da = da + pieces[k] * table[A_AT + 4 * t + k]
            db = own * table[B_AT]
            for shift in range(1, 4):
                db = db + turned(own, shifts[shift]) * table[B_AT + shift]
            emit(t, v, wind(0, t) * da + wind(1, t) * db)


def main_kernel(
    base,
    neighbours,
    valence,
    cost,
    table,
    w_in,
    w_mid,
    w_out,
    state_hbm,
    winds_hbm,
    dyn_hbm,
    phys_hbm,
    low_hbm,
    high_hbm,
    state,
    winds,
    adv,
    dyn,
    phys,
    wi,
    wm,
    wo,
    edge_sum,
    edge_rows,
    edge_sent,
    plan_vmem,
    plan,
    most,
    plan_sem,
    w_sem,
    edge_sem,
    in_sem,
    out_sem,
):
    def copies(s):
        at = pl.ds(s * RIB, RIB)
        return (
            pltpu.make_async_copy(state_hbm.at[at], state.at[at], in_sem.at[0, s]),
            pltpu.make_async_copy(winds_hbm.at[0, at], winds.at[0, at], in_sem.at[1, s]),
            pltpu.make_async_copy(winds_hbm.at[1, at], winds.at[1, at], in_sem.at[2, s]),
        )

    def fetch(s):
        for copy in copies(s):
            copy.start()

    def arrive(s):
        for copy in copies(s):
            copy.wait()

    fetch(0)
    fetch(SWEEPS - 1)
    loads = [
        pltpu.make_async_copy(w_in, wi, w_sem.at[0]),
        pltpu.make_async_copy(w_mid, wm.at[pl.ds(0, 3)], w_sem.at[1]),
        pltpu.make_async_copy(w_out, wo, w_sem.at[2]),
    ]
    for copy in loads:
        copy.start()
    for s in range(1, SWEEPS - 1):
        fetch(s)
    plan_vmem[0:8, :] = ((neighbours[...] - base[0] + RIB) & (ALL - 1)) * 16
    corner = valence[...] - 3
    plan_vmem[8:9, :] = corner[3:4] * 4 + corner[2:3] * 2 + W_AT
    plan_vmem[9:10, :] = corner[1:2] * 4 + corner[0:1] * 2 + W_AT + 8
    plan_vmem[10:16, :] = jnp.zeros((6, 128), jnp.int32)
    send_plan = pltpu.make_async_copy(plan_vmem, plan, plan_sem)
    send_plan.start()
    edge_sum[...] = jnp.zeros(edge_sum.shape, F32)

    for v in range(4):
        adv[v, : 16 * RIB, :] = jnp.zeros((16 * RIB, 128), F32)
        adv[v, 16 * RIB * (SWEEPS + 1) : 16 * RIB * (SWEEPS + 2), :] = jnp.zeros(
            (16 * RIB, 128), F32
        )
    costs = lax.dot_general(
        cost[...].astype(BF16),
        (
            lax.broadcasted_iota(jnp.int32, (16, 16), 0)
            == lax.broadcasted_iota(jnp.int32, (16, 16), 1)
        ).astype(BF16),
        (((0,), (0,)), ((), ())),
        preferred_element_type=F32,
    )

    def advect(e, to, halves=(0, 1), emit=None):
        def keep(t, v, value):
            adv[v, pl.ds(pl.multiple_of(to * 16 + 8 * t, 8), 8), :] = value
            if emit is not None:
                emit(t, v, value)

        element_advect(
            lambda t, v: state[e, 8 * t : 8 * t + 8, 128 * v : 128 * (v + 1)],
            lambda d, t: winds[d, e, 8 * t : 8 * t + 8, :],
            table,
            halves,
            keep,
        )

    def assemble(e):
        sub = sublanes()
        along = sub % 4
        at = [plan[c, e] for c in range(8)]
        own_at = pl.multiple_of((e + RIB) * 16, 16)
        for t in range(2):
            entry = plan[8 + t, e]
            weight = table[entry]
            corner = table[entry + 1]
            for v in range(4):

                def rows(start):
                    return adv[v, pl.ds(start, 8), :]

                if t == 0:
                    across = jnp.where(sub < 4, rows(at[1] + 12), 0.0)
                    diagonal = jnp.where(sub == 0, rows(at[7] + 15), rows(at[6] + 9))
                else:
                    across = jnp.where(sub >= 4, rows(at[0] - 4), 0.0)
                    diagonal = jnp.where(sub == 4, rows(at[5] - 1), rows(at[4] - 7))
                beside = jnp.where(
                    along == 3,
                    rows(at[2] + 8 * t - 3),
                    jnp.where(along == 0, rows(at[3] + 8 * t + 3), 0.0),
                )
                own = adv[v, pl.ds(own_at + 8 * t, 8), :]
                dyn[e, 8 * t : 8 * t + 8, 128 * v : 128 * (v + 1)] = (
                    own + across + beside
                ) * weight + diagonal * corner

    def network(first_element, counts, substeps):
        x = state[pl.ds(first_element, RIB)].reshape(16 * RIB, 512).astype(BF16)
        a = dot(x, wi[...])
        yield a[:8, :128]
        total = None
        for s in range(substeps):
            h = silu_half(a)
            for k in range(3):
                pre = dot(h, wm[k])
                yield pre[:8, :128]
                h = silu_half(pre)
            wide = h.astype(F32)
            if s == 0:
                total = wide
            else:
                active = counts > s
                total = total + jnp.concatenate(
                    [
                        jnp.where(active, wide[:, 128 * v : 128 * (v + 1)], 0.0)
                        for v in range(3)
                    ],
                    1,
                )
            if s < substeps - 1:
                a = a + dot(h, wm[3])
                yield a[:8, :128]
        tend = dot(total.astype(BF16), wo[...])
        phys[pl.ds(first_element, RIB)] = tend.astype(BF16).reshape(RIB, 16, 512)

    for t in range(STEPS):
        most[t] = jnp.max(cost[:, 32 * t : 32 * t + 32])

    def column_counts(first_element):
        block = costs_ref(first_element)
        spread = jnp.broadcast_to(block[:, None, :], (RIB, 16, 16))
        point = lax.broadcasted_iota(jnp.int32, (RIB, 16, 16), 1)
        lane = lax.broadcasted_iota(jnp.int32, (RIB, 16, 16), 2)
        spread = jnp.where(point == lane, spread, 0.0).reshape(16 * RIB, 16)
        return dot(spread.astype(BF16), jnp.ones((16, 128), BF16))

    for s in range(SWEEPS):
        winds[0, RIB * SWEEPS + s, :, 0:16] = costs[s * RIB : (s + 1) * RIB]

    def costs_ref(first_element):
        return winds[0, RIB * SWEEPS + first_element // RIB, :, 0:16]

    def results(t):
        at = pl.ds(t * 2 * RIB, 2 * RIB)
        return (
            pltpu.make_async_copy(dyn.at[at], dyn_hbm.at[at], out_sem.at[0, t]),
            pltpu.make_async_copy(phys.at[at], phys_hbm.at[at], out_sem.at[1, t]),
        )

    send_plan.wait()
    arrive(0)
    arrive(SWEEPS - 1)
    sub = sublanes()
    swap = sub ^ 4

    def contribute(k, e):
        slots = (0, 5, 4) if k else (1, 7, 6)
        origin = RIB * (SWEEPS + 1) if k else 0
        at = [(plan[c, e] >> 4) - origin for c in slots]
        entry = plan[8 + k, e]
        weight, corner = table[entry], table[entry + 1]
        own = 4 * k
        far = 4 - own

        def emit(t, v, value):
            if t != k:
                return
            lanes = slice(128 * v, 128 * (v + 1))
            edge = turned(value * weight, swap)
            edge_sum[k, at[0], :, lanes] += jnp.where((sub >= far) & (sub < far + 4), edge, 0.0)
            diagonal = value * corner
            edge_sum[k, at[1], :, lanes] += jnp.where(
                sub == far + 3, pltpu.roll(diagonal, (far + 3 - own) % 8, 0), 0.0
            )
            edge_sum[k, at[2], :, lanes] += jnp.where(
                sub == far, pltpu.roll(diagonal, (far - own - 3) % 8, 0), 0.0
            )

        return emit

    def edges(e, _):
        advect(e, e + RIB, emit=contribute(0, e))
        last = e + RIB * (SWEEPS - 1)
        advect(last, last + RIB, (1,), contribute(1, last))
        return 0

    lax.fori_loop(0, RIB, edges, 0, unroll=4)
    for m in range(RIB // 2):
        for v in range(4):
            lanes = slice(128 * v, 128 * (v + 1))
            for k in range(2):
                first, second = edge_sum[k, 2 * m, :, lanes], edge_sum[k, 2 * m + 1, :, lanes]
                first, second = (first, turned(second, swap)) if k else (turned(first, swap), second)
                edge_rows[k, 8 * m : 8 * m + 8, lanes] = jnp.where(sub < 4, first, second)
    edge_sent[...] = edge_rows[...].astype(BF16)
    sent = [
        pltpu.make_async_copy(edge_sent.at[0], low_hbm, edge_sem.at[0]),
        pltpu.make_async_copy(edge_sent.at[1], high_hbm, edge_sem.at[1]),
    ]
    for copy in sent:
        copy.start()
    for copy in loads:
        copy.wait()
    wm[3] = (dot(wo[...], wi[...]) * 0.5).astype(BF16)
    wi[...] = wi[...] * 0.5
    for k in range(3):
        wm[k] = wm[k] * 0.5

    def step(t, _):
        @pl.when(t < STEPS - 1)
        def _():
            arrive(2 * t + 1)
            arrive(2 * t + 2)

        def tasks():
            for e in range(32):
                number = t * 32 + RIB + e
                if e < RIB:
                    advect(number, number + RIB)
                else:
                    advect(
                        jnp.minimum(number, RIB * SWEEPS - RIB + e - RIB),
                        jnp.where(
                            t == STEPS - 1, RIB * (SWEEPS + 2) + e - RIB, number + RIB
                        ),
                    )
                    assemble(t * 32 + e - RIB)
                yield
            for e in range(RIB):
                assemble(t * 32 + RIB + e)
                yield

        def work(substeps):
            chains = [
                network(t * 32 + c * RIB, column_counts(t * 32 + c * RIB), substeps)
                for c in range(2)
            ]
            left = tasks()
            layers = 4 * substeps
            share = 0.0
            for _ in range(layers):
                for chain in chains:
                    pace = next(chain)
                    state[RIB * SWEEPS, 0:8, 0:128] = pace
                    adv[0, 16 * RIB * (SWEEPS + 3) :, :] = pace
                    share += 48 / (2 * layers)
                    while share >= 1.0:
                        next(left)
                        share -= 1.0
            for rest in (*chains, left):
                for _ in rest:
                    pass

        for substeps in range(1, SUB + 1):
            pl.when(most[t] == substeps)(functools.partial(work, substeps))
        for copy in results(t):
            copy.start()
        return 0

    lax.fori_loop(0, STEPS, step, 0)
    for copy in sent:
        copy.wait()
    for t in range(STEPS):
        for copy in results(t):
            copy.wait()


def halo_kernel(before_hbm, after_hbm, dyn_in, dyn_hbm, low, high, before, after, sem):
    last = RIB * (SWEEPS - 1)
    sub = sublanes()
    places = (
        (low, dyn_hbm.at[pl.ds(0, RIB), pl.ds(0, 8)]),
        (high, dyn_hbm.at[pl.ds(last, RIB), pl.ds(8, 8)]),
    )
    loads = [pltpu.make_async_copy(far, near, sem.at[k]) for k, (near, far) in enumerate(places)]
    stores = [
        pltpu.make_async_copy(near, far, sem.at[2 + k]) for k, (near, far) in enumerate(places)
    ]
    arrivals = [
        pltpu.make_async_copy(before_hbm, before, sem.at[4]),
        pltpu.make_async_copy(after_hbm, after, sem.at[5]),
    ]
    for copy in loads + arrivals:
        copy.start()
    for k, (near, halo) in enumerate(((low, before), (high, after))):
        loads[k].wait()
        arrivals[k].wait()
        kept = sub >= 4 if k else sub < 4
        for q in range(RIB // 4):
            packed = halo[16 * q : 16 * q + 16, :].astype(F32)
            for r in range(4):
                for v in range(4):
                    lanes = slice(128 * v, 128 * (v + 1))
                    tile = packed[8 * (r // 2) : 8 * (r // 2) + 8, lanes]
                    if r % 2 != k:
                        tile = pltpu.roll(tile, 4, 0)
                    near[4 * q + r, :, lanes] += jnp.where(kept, tile, 0.0)
        stores[k].start()
    for copy in stores:
        copy.wait()


def body(state, winds, neighbours, valence, cost, w_in, w_mid, w_out):
    vmem = pl.BlockSpec(memory_space=pltpu.VMEM)
    smem = pl.BlockSpec(memory_space=pltpu.SMEM)
    hbm = pl.BlockSpec(memory_space=pltpu.HBM)
    devices = lax.axis_size("dev")
    base = (lax.axis_index("dev") * (RIB * SWEEPS)).astype(jnp.int32).reshape(1)
    table = jnp.asarray(TABLE)
    edge = jax.ShapeDtypeStruct((RIB * 4, 512), BF16)
    dyn, phys, low, high = pl.pallas_call(
        main_kernel,
        out_shape=(
            jax.ShapeDtypeStruct(state.shape, F32),
            jax.ShapeDtypeStruct(state.shape, BF16),
            edge,
            edge,
        ),
        in_specs=[smem] + [vmem] * 4 + [hbm] * 5,
        out_specs=[hbm] * 4,
        scratch_shapes=[
            pltpu.VMEM((RIB * SWEEPS + 1, 16, 512), F32),
            pltpu.VMEM((2, RIB * SWEEPS + SWEEPS, 16, 128), F32),
            pltpu.VMEM((4, (SWEEPS + 3) * RIB * 16 + 8, 128), F32),
            pltpu.VMEM((RIB * SWEEPS, 16, 512), F32),
            pltpu.VMEM((RIB * SWEEPS, 16, 512), BF16),
            pltpu.VMEM(w_in.shape, BF16),
            pltpu.VMEM((4, 384, 384), BF16),
            pltpu.VMEM(w_out.shape, BF16),
            pltpu.VMEM((2, RIB, 8, 512), F32),
            pltpu.VMEM((2, RIB * 4, 512), F32),
            pltpu.VMEM((2, RIB * 4, 512), BF16),
            pltpu.VMEM((16, RIB * SWEEPS), jnp.int32),
            pltpu.SMEM((16, RIB * SWEEPS), jnp.int32),
            pltpu.SMEM((STEPS,), jnp.int32),
            pltpu.SemaphoreType.DMA(()),
            pltpu.SemaphoreType.DMA((3,)),
            pltpu.SemaphoreType.DMA((2,)),
            pltpu.SemaphoreType.DMA((3, SWEEPS)),
            pltpu.SemaphoreType.DMA((2, STEPS)),
        ],
        compiler_params=pltpu.CompilerParams(vmem_limit_bytes=63 * 2**20),
        cost_estimate=pl.CostEstimate(
            flops=12_000_000_000, bytes_accessed=14_000_000, transcendentals=10_000_000
        ),
    )(base, neighbours.T, valence.T, cost.T, table, w_in, w_mid, w_out, state, winds)
    forward = [(i, (i + 1) % devices) for i in range(devices)]
    backward = [(target, source) for source, target in forward]
    before = lax.ppermute(high, "dev", forward)
    after = lax.ppermute(low, "dev", backward)
    dyn = pl.pallas_call(
        halo_kernel,
        out_shape=jax.ShapeDtypeStruct(state.shape, F32),
        in_specs=[hbm] * 3,
        out_specs=hbm,
        scratch_shapes=[
            pltpu.VMEM((RIB, 8, 512), F32),
            pltpu.VMEM((RIB, 8, 512), F32),
            pltpu.VMEM((RIB * 4, 512), BF16),
            pltpu.VMEM((RIB * 4, 512), BF16),
            pltpu.SemaphoreType.DMA((6,)),
        ],
        input_output_aliases={2: 0},
        compiler_params=pltpu.CompilerParams(vmem_limit_bytes=63 * 2**20),
        cost_estimate=pl.CostEstimate(
            flops=1_000_000, bytes_accessed=2_000_000, transcendentals=0
        ),
    )(before, after, dyn)
    return dyn, phys


def solution(mesh):
    return jax.shard_map(
        body,
        mesh=mesh,
        in_specs=(
            P("dev", None, None),
            P(None, "dev", None, None),
            P("dev", None),
            P("dev", None),
            P("dev", None),
            P(),
            P(),
            P(),
        ),
        out_specs=(P("dev", None, None), P("dev", None, None)),
        check_vma=False,
    )
```

```python
import functools

import jax
import jax.numpy as jnp
import numpy as np
from jax import lax
from jax.experimental import pallas as pl
from jax.experimental.pallas import tpu as pltpu
from jax.sharding import PartitionSpec as P

RIB = 16
SUB = 4
SWEEPS = 8
STEPS = 4
ALL = 16384
F32 = jnp.float32
BF16 = jnp.bfloat16


def lobatto_table():
    nodes = np.array([-1.0, -1.0 / np.sqrt(5.0), 1.0 / np.sqrt(5.0), 1.0])
    weights = np.array(
        [
            1.0 / np.prod([nodes[outer] - nodes[inner] for inner in range(4) if inner != outer])
            for outer in range(4)
        ]
    )
    deriv = np.zeros((4, 4))
    for outer in range(4):
        for inner in range(4):
            if inner != outer:
                deriv[outer, inner] = weights[inner] / weights[outer] / (nodes[outer] - nodes[inner])
        deriv[outer, outer] = -np.sum(deriv[outer])
    return deriv.astype(np.float32)


def constant_table():
    deriv = lobatto_table()
    sub = np.arange(8)
    half, along = sub // 4, sub % 4
    rows = []
    for t in range(2):
        i = 2 * t + half
        for source in (half, 1 - half, 2 + half, 3 - half):
            rows.append(-deriv[i, source])
    for shift in range(4):
        rows.append(-deriv[along, (along + shift) % 4])
    for t in range(2):
        first, second = (0, 3) if t == 0 else (4, 7)
        edge = np.ones(8)
        edge += (half == t) * 1.0
        edge += (along == 0) * 1.0
        edge += (along == 3) * 1.0
        for pattern in range(4):
            present = np.zeros(8)
            present[first] = pattern // 2
            present[second] = pattern % 2
            rows.append(1.0 / (edge + present))
            rows.append(present / (edge + present))
    table = np.stack(rows).astype(np.float32)
    return np.ascontiguousarray(np.broadcast_to(table[:, :, None], table.shape + (128,)))


TABLE = constant_table()
A_AT, B_AT, W_AT = 0, 8, 12


def dot(a, b):
    return jnp.dot(a, b, preferred_element_type=F32)


def silu_half(h):
    h = h.astype(BF16)
    return h + h * jnp.tanh(h)


def sublanes():
    return lax.broadcasted_iota(jnp.int32, (8, 128), 0)


def turned(tile, pattern):
    return jnp.take_along_axis(tile, pattern, axis=0, mode="promise_in_bounds")


def element_advect(load, wind, table, halves, emit):
    sub = sublanes()
    swap = sub ^ 4
    shifts = [(sub & 4) | ((sub + shift) & 3) for shift in range(4)]
    for v in range(4):
        low, high = load(0, v), load(1, v)
        pieces = (low, turned(low, swap), high, turned(high, swap))
        for t in halves:
            own = (low, high)[t]
            da = pieces[0] * table[A_AT + 4 * t]
            for k in range(1, 4):
                da = da + pieces[k] * table[A_AT + 4 * t + k]
            db = own * table[B_AT]
            for shift in range(1, 4):
                db = db + turned(own, shifts[shift]) * table[B_AT + shift]
            emit(t, v, wind(0, t) * da + wind(1, t) * db)


def main_kernel(
    base,
    neighbours_hbm,
    valence_hbm,
    cost_hbm,
    table_hbm,
    w_in,
    w_mid,
    w_out,
    state_hbm,
    winds_hbm,
    dyn_hbm,
    phys_hbm,
    low_hbm,
    high_hbm,
    neighbours,
    valence,
    cost,
    table,
    state,
    winds,
    adv,
    dyn,
    phys,
    wi,
    wm,
    wo,
    edge_sum,
    edge_rows,
    edge_sent,
    plan_vmem,
    plan,
    most,
    plan_sem,
    small_sem,
    w_sem,
    edge_sem,
    in_sem,
    out_sem,
):
    def copies(s):
        at = pl.ds(s * RIB, RIB)
        return (
            pltpu.make_async_copy(state_hbm.at[at], state.at[at], in_sem.at[0, s]),
            pltpu.make_async_copy(winds_hbm.at[0, at], winds.at[0, at], in_sem.at[1, s]),
            pltpu.make_async_copy(winds_hbm.at[1, at], winds.at[1, at], in_sem.at[2, s]),
        )

    def fetch(s):
        for copy in copies(s):
            copy.start()

    def arrive(s):
        for copy in copies(s):
            copy.wait()

    small = [
        pltpu.make_async_copy(neighbours_hbm, neighbours, small_sem.at[0]),
        pltpu.make_async_copy(valence_hbm, valence, small_sem.at[1]),
        pltpu.make_async_copy(table_hbm, table, small_sem.at[2]),
        pltpu.make_async_copy(cost_hbm, cost, small_sem.at[3]),
    ]
    for copy in small:
        copy.start()
    fetch(0)
    fetch(SWEEPS - 1)
    loads = [
        pltpu.make_async_copy(w_in, wi, w_sem.at[0]),
        pltpu.make_async_copy(w_mid, wm.at[pl.ds(0, 3)], w_sem.at[1]),
        pltpu.make_async_copy(w_out, wo, w_sem.at[2]),
    ]
    for copy in loads:
        copy.start()
    for s in range(1, SWEEPS - 1):
        fetch(s)
    for v in range(4):
        adv[v, : 16 * RIB, :] = jnp.zeros((16 * RIB, 128), F32)
        adv[v, 16 * RIB * (SWEEPS + 1) : 16 * RIB * (SWEEPS + 2), :] = jnp.zeros(
            (16 * RIB, 128), F32
        )
    for copy in small:
        copy.wait()
    plan_vmem[0:8, :] = ((neighbours[...] - base[0] + RIB) & (ALL - 1)) * 16
    corner = valence[...] - 3
    plan_vmem[8:9, :] = corner[3:4] * 4 + corner[2:3] * 2 + W_AT
    plan_vmem[9:10, :] = corner[1:2] * 4 + corner[0:1] * 2 + W_AT + 8
    plan_vmem[10:16, :] = jnp.zeros((6, 128), jnp.int32)
    send_plan = pltpu.make_async_copy(plan_vmem, plan, plan_sem)
    send_plan.start()
    costs = lax.dot_general(
        cost[...].astype(BF16),
        (
            lax.broadcasted_iota(jnp.int32, (16, 16), 0)
            == lax.broadcasted_iota(jnp.int32, (16, 16), 1)
        ).astype(BF16),
        (((0,), (0,)), ((), ())),
        preferred_element_type=F32,
    )

    def advect(e, to, halves=(0, 1), emit=None):
        def keep(t, v, value):
            adv[v, pl.ds(pl.multiple_of(to * 16 + 8 * t, 8), 8), :] = value
            if emit is not None:
                emit(t, v, value)

        element_advect(
            lambda t, v: state[e, 8 * t : 8 * t + 8, 128 * v : 128 * (v + 1)],
            lambda d, t: winds[d, e, 8 * t : 8 * t + 8, :],
            table,
            halves,
            keep,
        )

    def assemble(e):
        sub = sublanes()
        along = sub % 4
        at = [plan[c, e] for c in range(8)]
        own_at = pl.multiple_of((e + RIB) * 16, 16)
        for t in range(2):
            entry = plan[8 + t, e]
            weight = table[entry]
            corner = table[entry + 1]
            for v in range(4):

                def rows(start):
                    return adv[v, pl.ds(start, 8), :]

                if t == 0:
                    across = jnp.where(sub < 4, rows(at[1] + 12), 0.0)
                    diagonal = jnp.where(sub == 0, rows(at[7] + 15), rows(at[6] + 9))
                else:
                    across = jnp.where(sub >= 4, rows(at[0] - 4), 0.0)
                    diagonal = jnp.where(sub == 4, rows(at[5] - 1), rows(at[4] - 7))
                beside = jnp.where(
                    along == 3,
                    rows(at[2] + 8 * t - 3),
                    jnp.where(along == 0, rows(at[3] + 8 * t + 3), 0.0),
                )
                own = adv[v, pl.ds(own_at + 8 * t, 8), :]
                dyn[e, 8 * t : 8 * t + 8, 128 * v : 128 * (v + 1)] = (
                    own + across + beside
                ) * weight + diagonal * corner

    def network(first_element, counts, substeps):
        x = state[pl.ds(first_element, RIB)].reshape(16 * RIB, 512).astype(BF16)
        a = dot(x, wi[...])
        yield a[:8, :128]
        total = None
        for s in range(substeps):
            h = silu_half(a)
            for k in range(3):
                pre = dot(h, wm[k])
                yield pre[:8, :128]
                h = silu_half(pre)
            wide = h.astype(F32)
            if s == 0:
                total = wide
            else:
                active = counts > s
                total = total + jnp.concatenate(
                    [
                        jnp.where(active, wide[:, 128 * v : 128 * (v + 1)], 0.0)
                        for v in range(3)
                    ],
                    1,
                )
            if s < substeps - 1:
                a = a + dot(h, wm[3])
                yield a[:8, :128]
        tend = dot(total.astype(BF16), wo[...])
        phys[pl.ds(first_element, RIB)] = tend.astype(BF16).reshape(RIB, 16, 512)

    for t in range(STEPS):
        most[t] = jnp.max(cost[:, 32 * t : 32 * t + 32])

    def column_counts(first_element):
        block = costs_ref(first_element)
        spread = jnp.broadcast_to(block[:, None, :], (RIB, 16, 16))
        point = lax.broadcasted_iota(jnp.int32, (RIB, 16, 16), 1)
        lane = lax.broadcasted_iota(jnp.int32, (RIB, 16, 16), 2)
        spread = jnp.where(point == lane, spread, 0.0).reshape(16 * RIB, 16)
        return dot(spread.astype(BF16), jnp.ones((16, 128), BF16))

    for s in range(SWEEPS):
        winds[0, RIB * SWEEPS + s, :, 0:16] = costs[s * RIB : (s + 1) * RIB]

    def costs_ref(first_element):
        return winds[0, RIB * SWEEPS + first_element // RIB, :, 0:16]

    def results(t):
        at = pl.ds(t * 2 * RIB, 2 * RIB)
        return (
            pltpu.make_async_copy(dyn.at[at], dyn_hbm.at[at], out_sem.at[0, t]),
            pltpu.make_async_copy(phys.at[at], phys_hbm.at[at], out_sem.at[1, t]),
        )

    send_plan.wait()
    arrive(0)
    arrive(SWEEPS - 1)
    sub = sublanes()
    swap = sub ^ 4

    def contribute(k, e):
        slots = (0, 5, 4) if k else (1, 7, 6)
        origin = RIB * (SWEEPS + 1) if k else 0
        at = [(plan[c, e] >> 4) - origin for c in slots]
        entry = plan[8 + k, e]
        weight, corner = table[entry], table[entry + 1]
        own = 4 * k
        far = 4 - own

        def emit(t, v, value):
            if t != k:
                return
            lanes = slice(128 * v, 128 * (v + 1))
            edge = turned(value * weight, swap)
            edge_sum[k, 0, at[0], :, lanes] = edge
            diagonal = value * corner
            edge_sum[k, 1, at[1], :, lanes] = pltpu.roll(diagonal, (far + 3 - own) % 8, 0)
            edge_sum[k, 2, at[2], :, lanes] = pltpu.roll(diagonal, (far - own - 3) % 8, 0)

        return emit

    def edges(e, _):
        advect(e, e + RIB, emit=contribute(0, e))
        last = e + RIB * (SWEEPS - 1)
        advect(last, last + RIB, (1,), contribute(1, last))
        return 0

    lax.fori_loop(0, RIB, edges, 0, unroll=4)
    for m in range(RIB // 2):
        for v in range(4):
            lanes = slice(128 * v, 128 * (v + 1))
            for k in range(2):
                far = 0 if k else 4
                first, second = [
                    edge_sum[k, 0, e, :, lanes]
                    + jnp.where(sub == far + 3, edge_sum[k, 1, e, :, lanes], 0.0)
                    + jnp.where(sub == far, edge_sum[k, 2, e, :, lanes], 0.0)
                    for e in (2 * m, 2 * m + 1)
                ]
                first, second = (first, turned(second, swap)) if k else (turned(first, swap), second)
                edge_rows[k, 8 * m : 8 * m + 8, lanes] = jnp.where(sub < 4, first, second)
    edge_sent[...] = edge_rows[...].astype(BF16)
    sent = [
        pltpu.make_async_copy(edge_sent.at[0], low_hbm, edge_sem.at[0]),
        pltpu.make_async_copy(edge_sent.at[1], high_hbm, edge_sem.at[1]),
    ]
    for copy in sent:
        copy.start()
    for copy in loads:
        copy.wait()
    wm[3] = (dot(wo[...], wi[...]) * 0.5).astype(BF16)
    wi[...] = wi[...] * 0.5
    for k in range(3):
        wm[k] = wm[k] * 0.5

    def step(t, _):
        @pl.when(t < STEPS - 1)
        def _():
            arrive(2 * t + 1)
            arrive(2 * t + 2)

        def tasks():
            for e in range(32):
                number = t * 32 + RIB + e
                if e < RIB:
                    advect(number, number + RIB)
                else:
                    advect(
                        jnp.minimum(number, RIB * SWEEPS - RIB + e - RIB),
                        jnp.where(
                            t == STEPS - 1, RIB * (SWEEPS + 2) + e - RIB, number + RIB
                        ),
                    )
                    assemble(t * 32 + e - RIB)
                yield
            for e in range(RIB):
                assemble(t * 32 + RIB + e)
                yield

        def work(substeps):
            chains = [
                network(t * 32 + c * RIB, column_counts(t * 32 + c * RIB), substeps)
                for c in range(2)
            ]
            left = tasks()
            layers = 4 * substeps
            share = 0.0
            for _ in range(layers):
                for chain in chains:
                    pace = next(chain)
                    state[RIB * SWEEPS, 0:8, 0:128] = pace
                    adv[0, 16 * RIB * (SWEEPS + 3) :, :] = pace
                    share += 48 / (2 * layers)
                    while share >= 1.0:
                        next(left)
                        share -= 1.0
            for rest in (*chains, left):
                for _ in rest:
                    pass

        for substeps in range(1, SUB + 1):
            pl.when(most[t] == substeps)(functools.partial(work, substeps))
        for copy in results(t):
            copy.start()
        return 0

    lax.fori_loop(0, STEPS, step, 0)
    for copy in sent:
        copy.wait()
    for t in range(STEPS):
        for copy in results(t):
            copy.wait()


def halo_kernel(before_hbm, after_hbm, dyn_in, dyn_hbm, low, high, before, after, sem):
    last = RIB * (SWEEPS - 1)
    sub = sublanes()
    places = (
        (low, dyn_hbm.at[pl.ds(0, RIB), pl.ds(0, 8)]),
        (high, dyn_hbm.at[pl.ds(last, RIB), pl.ds(8, 8)]),
    )
    loads = [pltpu.make_async_copy(far, near, sem.at[k]) for k, (near, far) in enumerate(places)]
    stores = [
        pltpu.make_async_copy(near, far, sem.at[2 + k]) for k, (near, far) in enumerate(places)
    ]
    arrivals = [
        pltpu.make_async_copy(before_hbm, before, sem.at[4]),
        pltpu.make_async_copy(after_hbm, after, sem.at[5]),
    ]
    for copy in loads + arrivals:
        copy.start()
    for k, (near, halo) in enumerate(((low, before), (high, after))):
        loads[k].wait()
        arrivals[k].wait()
        kept = sub >= 4 if k else sub < 4
        for q in range(RIB // 4):
            packed = halo[16 * q : 16 * q + 16, :].astype(F32)
            for r in range(4):
                for v in range(4):
                    lanes = slice(128 * v, 128 * (v + 1))
                    tile = packed[8 * (r // 2) : 8 * (r // 2) + 8, lanes]
                    if r % 2 != k:
                        tile = pltpu.roll(tile, 4, 0)
                    near[4 * q + r, :, lanes] += jnp.where(kept, tile, 0.0)
        stores[k].start()
    for copy in stores:
        copy.wait()


def body(state, winds, neighbours, valence, cost, w_in, w_mid, w_out):
    smem = pl.BlockSpec(memory_space=pltpu.SMEM)
    hbm = pl.BlockSpec(memory_space=pltpu.HBM)
    devices = lax.axis_size("dev")
    base = (lax.axis_index("dev") * (RIB * SWEEPS)).astype(jnp.int32).reshape(1)
    table = jnp.asarray(TABLE)
    edge = jax.ShapeDtypeStruct((RIB * 4, 512), BF16)
    dyn, phys, low, high = pl.pallas_call(
        main_kernel,
        out_shape=(
            jax.ShapeDtypeStruct(state.shape, F32),
            jax.ShapeDtypeStruct(state.shape, BF16),
            edge,
            edge,
        ),
        in_specs=[smem] + [hbm] * 9,
        out_specs=[hbm] * 4,
        scratch_shapes=[
            pltpu.VMEM((8, RIB * SWEEPS), jnp.int32),
            pltpu.VMEM((4, RIB * SWEEPS), jnp.int32),
            pltpu.VMEM((16, RIB * SWEEPS), jnp.int32),
            pltpu.VMEM(TABLE.shape, F32),
            pltpu.VMEM((RIB * SWEEPS + 1, 16, 512), F32),
            pltpu.VMEM((2, RIB * SWEEPS + SWEEPS, 16, 128), F32),
            pltpu.VMEM((4, (SWEEPS + 3) * RIB * 16 + 8, 128), F32),
            pltpu.VMEM((RIB * SWEEPS, 16, 512), F32),
            pltpu.VMEM((RIB * SWEEPS, 16, 512), BF16),
            pltpu.VMEM(w_in.shape, BF16),
            pltpu.VMEM((4, 384, 384), BF16),
            pltpu.VMEM(w_out.shape, BF16),
            pltpu.VMEM((2, 3, RIB, 8, 512), F32),
            pltpu.VMEM((2, RIB * 4, 512), F32),
            pltpu.VMEM((2, RIB * 4, 512), BF16),
            pltpu.VMEM((16, RIB * SWEEPS), jnp.int32),
            pltpu.SMEM((16, RIB * SWEEPS), jnp.int32),
            pltpu.SMEM((STEPS,), jnp.int32),
            pltpu.SemaphoreType.DMA(()),
            pltpu.SemaphoreType.DMA((4,)),
            pltpu.SemaphoreType.DMA((3,)),
            pltpu.SemaphoreType.DMA((2,)),
            pltpu.SemaphoreType.DMA((3, SWEEPS)),
            pltpu.SemaphoreType.DMA((2, STEPS)),
        ],
        compiler_params=pltpu.CompilerParams(vmem_limit_bytes=63 * 2**20),
        cost_estimate=pl.CostEstimate(
            flops=12_000_000_000, bytes_accessed=14_000_000, transcendentals=10_000_000
        ),
    )(base, neighbours.T, valence.T, cost.T, table, w_in, w_mid, w_out, state, winds)
    forward = [(i, (i + 1) % devices) for i in range(devices)]
    backward = [(target, source) for source, target in forward]
    before = lax.ppermute(high, "dev", forward)
    after = lax.ppermute(low, "dev", backward)
    dyn = pl.pallas_call(
        halo_kernel,
        out_shape=jax.ShapeDtypeStruct(state.shape, F32),
        in_specs=[hbm] * 3,
        out_specs=hbm,
        scratch_shapes=[
            pltpu.VMEM((RIB, 8, 512), F32),
            pltpu.VMEM((RIB, 8, 512), F32),
            pltpu.VMEM((RIB * 4, 512), BF16),
            pltpu.VMEM((RIB * 4, 512), BF16),
            pltpu.SemaphoreType.DMA((6,)),
        ],
        input_output_aliases={2: 0},
        compiler_params=pltpu.CompilerParams(vmem_limit_bytes=63 * 2**20),
        cost_estimate=pl.CostEstimate(
            flops=1_000_000, bytes_accessed=2_000_000, transcendentals=0
        ),
    )(before, after, dyn)
    return dyn, phys


def solution(mesh):
    return jax.shard_map(
        body,
        mesh=mesh,
        in_specs=(
            P("dev", None, None),
            P(None, "dev", None, None),
            P("dev", None),
            P("dev", None),
            P("dev", None),
            P(),
            P(),
            P(),
        ),
        out_specs=(P("dev", None, None), P("dev", None, None)),
        check_vma=False,
    )
```

```python
import functools

import jax
import jax.numpy as jnp
import numpy as np
from jax import lax
from jax.experimental import pallas as pl
from jax.experimental.pallas import tpu as pltpu
from jax.sharding import PartitionSpec as P

RIB = 16
SUB = 4
SWEEPS = 8
STEPS = 4
ALL = 16384
F32 = jnp.float32
BF16 = jnp.bfloat16


def lobatto_table():
    nodes = np.array([-1.0, -1.0 / np.sqrt(5.0), 1.0 / np.sqrt(5.0), 1.0])
    weights = np.array(
        [
            1.0 / np.prod([nodes[outer] - nodes[inner] for inner in range(4) if inner != outer])
            for outer in range(4)
        ]
    )
    deriv = np.zeros((4, 4))
    for outer in range(4):
        for inner in range(4):
            if inner != outer:
                deriv[outer, inner] = weights[inner] / weights[outer] / (nodes[outer] - nodes[inner])
        deriv[outer, outer] = -np.sum(deriv[outer])
    return deriv.astype(np.float32)


def constant_table():
    deriv = lobatto_table()
    sub = np.arange(8)
    half, along = sub // 4, sub % 4
    rows = []
    for t in range(2):
        i = 2 * t + half
        for source in (half, 1 - half, 2 + half, 3 - half):
            rows.append(-deriv[i, source])
    for shift in range(4):
        rows.append(-deriv[along, (along + shift) % 4])
    for t in range(2):
        first, second = (0, 3) if t == 0 else (4, 7)
        edge = np.ones(8)
        edge += (half == t) * 1.0
        edge += (along == 0) * 1.0
        edge += (along == 3) * 1.0
        for pattern in range(4):
            present = np.zeros(8)
            present[first] = pattern // 2
            present[second] = pattern % 2
            rows.append(1.0 / (edge + present))
            rows.append(present / (edge + present))
    table = np.stack(rows).astype(np.float32)
    return np.ascontiguousarray(np.broadcast_to(table[:, :, None], table.shape + (128,)))


TABLE = constant_table()
A_AT, B_AT, W_AT = 0, 8, 12


def dot(a, b):
    return jnp.dot(a, b, preferred_element_type=F32)


def silu_half(h):
    h = h.astype(BF16)
    return h + h * jnp.tanh(h)


def sublanes():
    return lax.broadcasted_iota(jnp.int32, (8, 128), 0)


def turned(tile, pattern):
    return jnp.take_along_axis(tile, pattern, axis=0, mode="promise_in_bounds")


def element_advect(load, wind, table, halves, emit):
    sub = sublanes()
    swap = sub ^ 4
    shifts = [(sub & 4) | ((sub + shift) & 3) for shift in range(4)]
    for v in range(4):
        low, high = load(0, v), load(1, v)
        pieces = (low, turned(low, swap), high, turned(high, swap))
        for t in halves:
            own = (low, high)[t]
            da = pieces[0] * table[A_AT + 4 * t]
            for k in range(1, 4):
                da = da + pieces[k] * table[A_AT + 4 * t + k]
            db = own * table[B_AT]
            for shift in range(1, 4):
                db = db + turned(own, shifts[shift]) * table[B_AT + shift]
            emit(t, v, wind(0, t) * da + wind(1, t) * db)


def main_kernel(
    base,
    neighbours_hbm,
    valence_hbm,
    cost_hbm,
    table_hbm,
    w_in,
    w_mid,
    w_out,
    state_hbm,
    winds_hbm,
    dyn_hbm,
    phys_hbm,
    low_hbm,
    high_hbm,
    neighbours,
    valence,
    cost,
    table,
    state,
    winds,
    adv,
    dyn,
    phys,
    wi,
    wm,
    wo,
    edge_sum,
    edge_rows,
    edge_sent,
    plan_vmem,
    plan,
    most,
    plan_sem,
    small_sem,
    w_sem,
    edge_sem,
    in_sem,
    out_sem,
):
    def copies(s):
        at = pl.ds(s * RIB, RIB)
        return (
            pltpu.make_async_copy(state_hbm.at[at], state.at[at], in_sem.at[0, s]),
            pltpu.make_async_copy(winds_hbm.at[0, at], winds.at[0, at], in_sem.at[1, s]),
            pltpu.make_async_copy(winds_hbm.at[1, at], winds.at[1, at], in_sem.at[2, s]),
        )

    def fetch(s):
        for copy in copies(s):
            copy.start()

    def arrive(s):
        for copy in copies(s):
            copy.wait()

    small = [
        pltpu.make_async_copy(neighbours_hbm, neighbours, small_sem.at[0]),
        pltpu.make_async_copy(valence_hbm, valence, small_sem.at[1]),
        pltpu.make_async_copy(table_hbm, table, small_sem.at[2]),
        pltpu.make_async_copy(cost_hbm, cost, small_sem.at[3]),
    ]
    for copy in small:
        copy.start()
    fetch(0)
    fetch(SWEEPS - 1)
    loads = [
        pltpu.make_async_copy(w_in, wi, w_sem.at[0]),
        pltpu.make_async_copy(w_mid, wm.at[pl.ds(0, 3)], w_sem.at[1]),
        pltpu.make_async_copy(w_out, wo, w_sem.at[2]),
    ]
    for copy in loads:
        copy.start()
    for s in range(1, SWEEPS - 1):
        fetch(s)
    for v in range(4):
        adv[v, : 16 * RIB, :] = jnp.zeros((16 * RIB, 128), F32)
        adv[v, 16 * RIB * (SWEEPS + 1) : 16 * RIB * (SWEEPS + 2), :] = jnp.zeros(
            (16 * RIB, 128), F32
        )
    for copy in small:
        copy.wait()
    plan_vmem[0:8, :] = ((neighbours[...] - base[0] + RIB) & (ALL - 1)) * 16
    corner = valence[...] - 3
    plan_vmem[8:9, :] = corner[3:4] * 4 + corner[2:3] * 2 + W_AT
    plan_vmem[9:10, :] = corner[1:2] * 4 + corner[0:1] * 2 + W_AT + 8
    plan_vmem[10:16, :] = jnp.zeros((6, 128), jnp.int32)
    send_plan = pltpu.make_async_copy(plan_vmem, plan, plan_sem)
    send_plan.start()
    costs = lax.dot_general(
        cost[...].astype(BF16),
        (
            lax.broadcasted_iota(jnp.int32, (16, 16), 0)
            == lax.broadcasted_iota(jnp.int32, (16, 16), 1)
        ).astype(BF16),
        (((0,), (0,)), ((), ())),
        preferred_element_type=F32,
    )

    def advect(e, to, halves=(0, 1), emit=None):
        def keep(t, v, value):
            adv[v, pl.ds(pl.multiple_of(to * 16 + 8 * t, 8), 8), :] = value
            if emit is not None:
                emit(t, v, value)

        element_advect(
            lambda t, v: state[e, 8 * t : 8 * t + 8, 128 * v : 128 * (v + 1)],
            lambda d, t: winds[d, e, 8 * t : 8 * t + 8, :],
            table,
            halves,
            keep,
        )

    def assemble(e):
        sub = sublanes()
        along = sub % 4
        at = [plan[c, e] for c in range(8)]
        own_at = pl.multiple_of((e + RIB) * 16, 16)
        for t in range(2):
            entry = plan[8 + t, e]
            weight = table[entry]
            corner = table[entry + 1]
            for v in range(4):

                def rows(start):
                    return adv[v, pl.ds(start, 8), :]

                if t == 0:
                    across = jnp.where(sub < 4, rows(at[1] + 12), 0.0)
                    diagonal = jnp.where(sub == 0, rows(at[7] + 15), rows(at[6] + 9))
                else:
                    across = jnp.where(sub >= 4, rows(at[0] - 4), 0.0)
                    diagonal = jnp.where(sub == 4, rows(at[5] - 1), rows(at[4] - 7))
                beside = jnp.where(
                    along == 3,
                    rows(at[2] + 8 * t - 3),
                    jnp.where(along == 0, rows(at[3] + 8 * t + 3), 0.0),
                )
                own = adv[v, pl.ds(own_at + 8 * t, 8), :]
                dyn[e, 8 * t : 8 * t + 8, 128 * v : 128 * (v + 1)] = (
                    own + across + beside
                ) * weight + diagonal * corner

    def network(first_element, counts, substeps):
        x = state[pl.ds(first_element, RIB)].reshape(16 * RIB, 512).astype(BF16)
        a = dot(x, wi[...])
        yield a[:8, :128]
        total = None
        for s in range(substeps):
            h = silu_half(a)
            for k in range(3):
                pre = dot(h, wm[k])
                yield pre[:8, :128]
                h = silu_half(pre)
            wide = h.astype(F32)
            if s == 0:
                total = wide
            else:
                active = counts > s
                total = total + jnp.concatenate(
                    [
                        jnp.where(active, wide[:, 128 * v : 128 * (v + 1)], 0.0)
                        for v in range(3)
                    ],
                    1,
                )
            if s < substeps - 1:
                a = a + dot(h, wm[3])
                yield a[:8, :128]
        tend = dot(total.astype(BF16), wo[...])
        phys[pl.ds(first_element, RIB)] = tend.astype(BF16).reshape(RIB, 16, 512)

    for t in range(STEPS):
        most[t] = jnp.max(cost[:, 32 * t : 32 * t + 32])

    def column_counts(first_element):
        block = costs_ref(first_element)
        spread = jnp.broadcast_to(block[:, None, :], (RIB, 16, 16))
        point = lax.broadcasted_iota(jnp.int32, (RIB, 16, 16), 1)
        lane = lax.broadcasted_iota(jnp.int32, (RIB, 16, 16), 2)
        spread = jnp.where(point == lane, spread, 0.0).reshape(16 * RIB, 16)
        return dot(spread.astype(BF16), jnp.ones((16, 128), BF16))

    for s in range(SWEEPS):
        winds[0, RIB * SWEEPS + s, :, 0:16] = costs[s * RIB : (s + 1) * RIB]

    def costs_ref(first_element):
        return winds[0, RIB * SWEEPS + first_element // RIB, :, 0:16]

    def results(t):
        at = pl.ds(t * 2 * RIB, 2 * RIB)
        return (
            pltpu.make_async_copy(dyn.at[at], dyn_hbm.at[at], out_sem.at[0, t]),
            pltpu.make_async_copy(phys.at[at], phys_hbm.at[at], out_sem.at[1, t]),
        )

    send_plan.wait()
    arrive(0)
    arrive(SWEEPS - 1)
    sub = sublanes()
    swap = sub ^ 4

    def contribute(k, e):
        slots = (0, 5, 4) if k else (1, 7, 6)
        origin = RIB * (SWEEPS + 1) if k else 0
        at = [(plan[c, e] >> 4) - origin for c in slots]
        entry = plan[8 + k, e]
        weight, corner = table[entry], table[entry + 1]
        own = 4 * k
        far = 4 - own

        def emit(t, v, value):
            if t != k:
                return
            lanes = slice(128 * v, 128 * (v + 1))
            edge = turned(value * weight, swap)
            edge_sum[k, 0, at[0], :, lanes] = edge
            diagonal = value * corner
            edge_sum[k, 1, at[1], :, lanes] = pltpu.roll(diagonal, (far + 3 - own) % 8, 0)
            edge_sum[k, 2, at[2], :, lanes] = pltpu.roll(diagonal, (far - own - 3) % 8, 0)

        return emit

    def edges(e, _):
        advect(e, e + RIB, emit=contribute(0, e))
        last = e + RIB * (SWEEPS - 1)
        advect(last, last + RIB, (1,), contribute(1, last))
        return 0

    lax.fori_loop(0, RIB, edges, 0, unroll=4)
    for m in range(RIB // 2):
        for v in range(4):
            lanes = slice(128 * v, 128 * (v + 1))
            for k in range(2):
                far = 0 if k else 4
                first, second = [
                    edge_sum[k, 0, e, :, lanes]
                    + jnp.where(sub == far + 3, edge_sum[k, 1, e, :, lanes], 0.0)
                    + jnp.where(sub == far, edge_sum[k, 2, e, :, lanes], 0.0)
                    for e in (2 * m, 2 * m + 1)
                ]
                first, second = (first, turned(second, swap)) if k else (turned(first, swap), second)
                edge_rows[k, 8 * m : 8 * m + 8, lanes] = jnp.where(sub < 4, first, second)
    edge_sent[...] = edge_rows[...].astype(BF16)
    sent = [
        pltpu.make_async_copy(edge_sent.at[0], low_hbm, edge_sem.at[0]),
        pltpu.make_async_copy(edge_sent.at[1], high_hbm, edge_sem.at[1]),
    ]
    for copy in sent:
        copy.start()
    for copy in loads:
        copy.wait()
    wm[3] = (dot(wo[...], wi[...]) * 0.5).astype(BF16)
    wi[...] = wi[...] * 0.5
    for k in range(3):
        wm[k] = wm[k] * 0.5

    def step(t, _):
        @pl.when(t < STEPS - 1)
        def _():
            arrive(2 * t + 1)
            arrive(2 * t + 2)

        def tasks():
            for e in range(32):
                number = t * 32 + RIB + e
                if e < RIB:
                    advect(number, number + RIB)
                else:
                    advect(
                        jnp.minimum(number, RIB * SWEEPS - RIB + e - RIB),
                        jnp.where(
                            t == STEPS - 1, RIB * (SWEEPS + 2) + e - RIB, number + RIB
                        ),
                    )
                    assemble(t * 32 + e - RIB)
                yield
            for e in range(RIB):
                assemble(t * 32 + RIB + e)
                yield

        def work(substeps):
            chains = [
                network(t * 32 + c * RIB, column_counts(t * 32 + c * RIB), substeps)
                for c in range(2)
            ]
            left = tasks()
            layers = 4 * substeps
            share = 0.0
            for _ in range(layers):
                for chain in chains:
                    pace = next(chain)
                    state[RIB * SWEEPS, 0:8, 0:128] = pace
                    adv[0, 16 * RIB * (SWEEPS + 3) :, :] = pace
                    share += 48 / (2 * layers)
                    while share >= 1.0:
                        next(left)
                        share -= 1.0
            for rest in (*chains, left):
                for _ in rest:
                    pass

        for substeps in range(1, SUB + 1):
            pl.when(most[t] == substeps)(functools.partial(work, substeps))
        for copy in results(t):
            copy.start()
        return 0

    lax.fori_loop(0, STEPS, step, 0)
    for copy in sent:
        copy.wait()
    for t in range(STEPS):
        for copy in results(t):
            copy.wait()


def halo_kernel(before, after, dyn_in, dyn_hbm, low, high, sem):
    last = RIB * (SWEEPS - 1)
    sub = sublanes()
    places = (
        (low, dyn_hbm.at[pl.ds(0, RIB), pl.ds(0, 8)]),
        (high, dyn_hbm.at[pl.ds(last, RIB), pl.ds(8, 8)]),
    )
    loads = [pltpu.make_async_copy(far, near, sem.at[k]) for k, (near, far) in enumerate(places)]
    stores = [
        pltpu.make_async_copy(near, far, sem.at[2 + k]) for k, (near, far) in enumerate(places)
    ]
    for copy in loads:
        copy.start()
    for k, (near, halo) in enumerate(((low, before), (high, after))):
        loads[k].wait()
        kept = sub >= 4 if k else sub < 4
        for q in range(RIB // 4):
            packed = halo[16 * q : 16 * q + 16, :].astype(F32)
            for r in range(4):
                for v in range(4):
                    lanes = slice(128 * v, 128 * (v + 1))
                    tile = packed[8 * (r // 2) : 8 * (r // 2) + 8, lanes]
                    if r % 2 != k:
                        tile = pltpu.roll(tile, 4, 0)
                    near[4 * q + r, :, lanes] += jnp.where(kept, tile, 0.0)
        stores[k].start()
    for copy in stores:
        copy.wait()


def body(state, winds, neighbours, valence, cost, w_in, w_mid, w_out):
    smem = pl.BlockSpec(memory_space=pltpu.SMEM)
    hbm = pl.BlockSpec(memory_space=pltpu.HBM)
    devices = lax.axis_size("dev")
    base = (lax.axis_index("dev") * (RIB * SWEEPS)).astype(jnp.int32).reshape(1)
    table = jnp.asarray(TABLE)
    edge = jax.ShapeDtypeStruct((RIB * 4, 512), BF16)
    dyn, phys, low, high = pl.pallas_call(
        main_kernel,
        out_shape=(
            jax.ShapeDtypeStruct(state.shape, F32),
            jax.ShapeDtypeStruct(state.shape, BF16),
            edge,
            edge,
        ),
        in_specs=[smem] + [hbm] * 9,
        out_specs=[hbm] * 4,
        scratch_shapes=[
            pltpu.VMEM((8, RIB * SWEEPS), jnp.int32),
            pltpu.VMEM((4, RIB * SWEEPS), jnp.int32),
            pltpu.VMEM((16, RIB * SWEEPS), jnp.int32),
            pltpu.VMEM(TABLE.shape, F32),
            pltpu.VMEM((RIB * SWEEPS + 1, 16, 512), F32),
            pltpu.VMEM((2, RIB * SWEEPS + SWEEPS, 16, 128), F32),
            pltpu.VMEM((4, (SWEEPS + 3) * RIB * 16 + 8, 128), F32),
            pltpu.VMEM((RIB * SWEEPS, 16, 512), F32),
            pltpu.VMEM((RIB * SWEEPS, 16, 512), BF16),
            pltpu.VMEM(w_in.shape, BF16),
            pltpu.VMEM((4, 384, 384), BF16),
            pltpu.VMEM(w_out.shape, BF16),
            pltpu.VMEM((2, 3, RIB, 8, 512), F32),
            pltpu.VMEM((2, RIB * 4, 512), F32),
            pltpu.VMEM((2, RIB * 4, 512), BF16),
            pltpu.VMEM((16, RIB * SWEEPS), jnp.int32),
            pltpu.SMEM((16, RIB * SWEEPS), jnp.int32),
            pltpu.SMEM((STEPS,), jnp.int32),
            pltpu.SemaphoreType.DMA(()),
            pltpu.SemaphoreType.DMA((4,)),
            pltpu.SemaphoreType.DMA((3,)),
            pltpu.SemaphoreType.DMA((2,)),
            pltpu.SemaphoreType.DMA((3, SWEEPS)),
            pltpu.SemaphoreType.DMA((2, STEPS)),
        ],
        compiler_params=pltpu.CompilerParams(vmem_limit_bytes=63 * 2**20),
        cost_estimate=pl.CostEstimate(
            flops=12_000_000_000, bytes_accessed=14_000_000, transcendentals=10_000_000
        ),
    )(base, neighbours.T, valence.T, cost.T, table, w_in, w_mid, w_out, state, winds)
    forward = [(i, (i + 1) % devices) for i in range(devices)]
    backward = [(target, source) for source, target in forward]
    before = lax.ppermute(high, "dev", forward)
    after = lax.ppermute(low, "dev", backward)
    dyn = pl.pallas_call(
        halo_kernel,
        out_shape=jax.ShapeDtypeStruct(state.shape, F32),
        in_specs=[pl.BlockSpec(memory_space=pltpu.VMEM)] * 2 + [hbm],
        out_specs=hbm,
        scratch_shapes=[
            pltpu.VMEM((RIB, 8, 512), F32),
            pltpu.VMEM((RIB, 8, 512), F32),
            pltpu.SemaphoreType.DMA((4,)),
        ],
        input_output_aliases={2: 0},
        compiler_params=pltpu.CompilerParams(vmem_limit_bytes=8 * 2**20),
        cost_estimate=pl.CostEstimate(
            flops=1_000_000, bytes_accessed=2_000_000, transcendentals=0
        ),
    )(before, after, dyn)
    return dyn, phys


def solution(mesh):
    return jax.shard_map(
        body,
        mesh=mesh,
        in_specs=(
            P("dev", None, None),
            P(None, "dev", None, None),
            P("dev", None),
            P("dev", None),
            P("dev", None),
            P(),
            P(),
            P(),
        ),
        out_specs=(P("dev", None, None), P("dev", None, None)),
        check_vma=False,
    )
```
